32 devices in a mesh: tile: 16 (over z, x, core), head: 2 (over y).
Axes of the slice: x: 2, y: 2, z: 4, core: 2. Of those that a mesh axis runs over, the one named last changes fastest.
Arguments:
- queries: bfloat16 [16384, 768], P(('tile', 'head')), may hold values from -16 to 16
- keys_in: bfloat16 [16384, 768], P(('tile', 'head')), may hold values from -16 to 16
- values_in: bfloat16 [16384, 768], P(('tile', 'head')), may hold values from -6 to 6
- grad_out: bfloat16 [16384, 768], P(('tile', 'head')), may hold values from -6 to 6
- positions: int32 [2, 16384], P(None, ('tile', 'head')), may hold values from 0 to 255
Outputs:
- attended: bfloat16 [16384, 768], P(('tile', 'head'))
- query_grad: bfloat16 [16384, 768], P(('tile', 'head'))
- key_grad: bfloat16 [16384, 768], P(('tile', 'head'))
- value_grad: bfloat16 [16384, 768], P(('tile', 'head'))
The draws below stay inside these ranges and needn't reach their ends.
All inputs are finite; a program needn't handle non-finite values.
Results may differ from the reference program's by a relative error of at most 0.011.
Values may be sent and summed in bfloat16 or wider, within the bound.
A program may use at most 128 MiB of HBM per device.

```python
import math
import jax
import jax.numpy as jnp
from jax import lax

HEAD_DIM = 128
WIDTH = 768
TILE_TOK = 256
GRID_COLS = 8
TILES = 64
GRID_ROWS = 8
TOKENS = 16384
POS_SPAN = 256


def draw_pair(key):
    shape_all = (TOKENS, WIDTH)
    query_part = jnp.clip(jax.random.normal(jax.random.fold_in(key, 31), shape_all), -6.0, 6.0)
    key_part = jnp.clip(jax.random.normal(jax.random.fold_in(key, 32), shape_all), -6.0, 6.0)
    return (query_part, key_part)


def draw_queries(key, part):
    return draw_pair(key)[0].astype(jnp.bfloat16)


def draw_keys_in(key, part):
    return draw_pair(key)[1].astype(jnp.bfloat16)


def set_ends(array, key, low, top_value):
    place = [jax.random.randint(jax.random.fold_in(key, axis), (), 0, length) for axis, length in enumerate(array.shape)]
    main_axis = array.shape.index(max(array.shape))
    neighbour = place[:main_axis] + [(place[main_axis] + 1) % array.shape[main_axis]] + place[main_axis + 1:]
    return array.at[tuple(place)].set(low).at[tuple(neighbour)].set(top_value)


def steps_of(rng, dims, cuts, smallest, top_value):
    loudness, own = 1.0, jax.random.fold_in(rng, 6)
    for axis_at, parts in cuts:
        draws = jnp.exp(jax.random.uniform(jax.random.fold_in(own, axis_at), (parts,), jnp.float32, smallest / len(cuts), top_value / len(cuts)))
        loudness = loudness * jnp.repeat(draws, dims[axis_at] // parts).reshape([-1 if axis == axis_at else 1 for axis in range(len(dims))])
    return loudness


def normal_values(stream_key, dims, deviation, bound, pieces=(), held_as=jnp.bfloat16):
    gain = steps_of(stream_key, dims, pieces, -0.22, 0.18) if pieces else 1.0
    entries = jax.random.normal(stream_key, dims, jnp.float32) * deviation * gain
    return jnp.minimum(jnp.maximum(entries, -bound), bound).astype(held_as)


def setup_inputs(seed: int = 0) -> dict:
    seeds = jax.random.split(jax.random.key(seed), 6)
    queries = draw_queries(jax.random.fold_in(seeds[5], 71), 0)
    keys_in = draw_keys_in(jax.random.fold_in(seeds[5], 71), 0)
    values_in = normal_values(seeds[2], (TOKENS, WIDTH), 1.0, 6.0, ((0, 32),))
    grad_out = normal_values(seeds[3], (TOKENS, WIDTH), 1.0, 6.0, ((0, 32),))
    positions = set_ends(jax.random.randint(seeds[4], (2, TOKENS), 0, POS_SPAN), jax.random.fold_in(seeds[4], 1), 0, POS_SPAN - 1).astype(jnp.int32)
    return dict(queries=queries, keys_in=keys_in, values_in=values_in, grad_out=grad_out, positions=positions)


THETA = 10000.0


def angle_tables(row_ids, col_ids):
    turned = 7 * HEAD_DIM // 16
    unturned = HEAD_DIM - 2 * turned
    slot_ids = lax.iota(jnp.int32, HEAD_DIM)
    offset = slot_ids - unturned
    by_column = offset >= turned
    within = jnp.where(by_column, offset - turned, offset)
    paired = jnp.maximum(within, 0) // 2
    frequency = jnp.exp(paired.astype(jnp.float32) * (-2.0 * math.log(THETA) / turned))
    chosen = jnp.where(by_column[None, :], col_ids[:, None], row_ids[:, None]).astype(jnp.float32)
    angles = chosen * frequency[None, :]
    active = (offset >= 0)[None, :]
    cosine = jnp.where(active, jnp.cos(angles), 1.0)
    parity = jnp.where(within % 2 == 0, -1.0, 1.0)
    signed_sine = jnp.where(active, jnp.sin(angles) * parity[None, :], 0.0)
    return cosine, signed_sine


def swap_matrix():
    slot_ids = lax.iota(jnp.int32, HEAD_DIM)
    partner = jnp.bitwise_xor(slot_ids, 1)
    return (slot_ids[:, None] == partner[None, :]).astype(jnp.float32)


def turn_forward(tensor, cosine, signed_sine, matrix):
    flattened = tensor.reshape(-1, HEAD_DIM)
    swapped = jnp.dot(flattened, matrix, precision=lax.Precision.HIGHEST).reshape(tensor.shape)
    return tensor * cosine[:, None, :] + swapped * signed_sine[:, None, :]


def turn_back(gradient, cosine, signed_sine, matrix):
    flattened = (gradient * signed_sine[:, None, :]).reshape(-1, HEAD_DIM)
    swapped = jnp.dot(flattened, matrix, precision=lax.Precision.HIGHEST).reshape(gradient.shape)
    return gradient * cosine[:, None, :] + swapped


def query_kernel(q_tile, g_tile, near_keys, near_values, usable):
    highest = lax.Precision.HIGHEST
    inv_root = HEAD_DIM ** -0.5
    scores = jnp.einsum("qhd,khd->hqk", q_tile.astype(jnp.float32), near_keys.astype(jnp.float32), precision=highest) * inv_root
    scores = jnp.where(usable[None, None, :], scores, -jnp.inf)
    row_max = jnp.max(scores, axis=-1, keepdims=True)
    log_norm = row_max + jnp.log(jnp.sum(jnp.exp(scores - row_max), axis=-1, keepdims=True))
    weights = jnp.exp(scores - log_norm)
    weights_half = lax.optimization_barrier(weights.astype(jnp.bfloat16))
    attended = jnp.einsum("hqk,khd->qhd", weights_half.astype(jnp.float32), near_values.astype(jnp.float32), precision=highest)
    attended = lax.optimization_barrier(attended.astype(jnp.bfloat16))
    row_dots = jnp.sum(g_tile.astype(jnp.float32) * attended.astype(jnp.float32), axis=-1).T
    weight_grad = jnp.einsum("qhd,khd->hqk", g_tile.astype(jnp.float32), near_values.astype(jnp.float32), precision=highest)
    dscore = lax.optimization_barrier((weights * (weight_grad - row_dots[:, :, None]) * inv_root).astype(jnp.bfloat16))
    dq_rot = jnp.einsum("hqk,khd->qhd", dscore.astype(jnp.float32), near_keys.astype(jnp.float32), precision=highest)
    return attended, log_norm[:, :, 0], row_dots, dq_rot


def key_kernel(k_tile, v_tile, near_queries, near_grads, near_norms, near_dots, usable):
    highest = lax.Precision.HIGHEST
    inv_root = HEAD_DIM ** -0.5
    scores = jnp.einsum("khd,qhd->hkq", k_tile.astype(jnp.float32), near_queries.astype(jnp.float32), precision=highest) * inv_root
    weights = jnp.where(usable[None, None, :], jnp.exp(scores - near_norms[:, None, :]), 0.0)
    weights_half = lax.optimization_barrier(weights.astype(jnp.bfloat16))
    dv_part = jnp.einsum("hkq,qhd->khd", weights_half.astype(jnp.float32), near_grads.astype(jnp.float32), precision=highest)
    weight_grad = jnp.einsum("khd,qhd->hkq", v_tile.astype(jnp.float32), near_grads.astype(jnp.float32), precision=highest)
    dscore = lax.optimization_barrier((weights * (weight_grad - near_dots[:, None, :]) * inv_root).astype(jnp.bfloat16))
    dk_part = jnp.einsum("hkq,qhd->khd", dscore.astype(jnp.float32), near_queries.astype(jnp.float32), precision=highest)
    return dk_part, dv_part


def reference(queries, keys_in, values_in, grad_out, positions):
    head_count = queries.shape[1] // HEAD_DIM
    shape_all = (TOKENS, head_count, HEAD_DIM)
    cosine, signed_sine = angle_tables(positions[0], positions[1])
    matrix = swap_matrix()
    q_rot = turn_forward(queries.astype(jnp.float32).reshape(shape_all), cosine, signed_sine, matrix)
    q_rot = lax.optimization_barrier(q_rot.astype(jnp.bfloat16))
    k_rot = turn_forward(keys_in.astype(jnp.float32).reshape(shape_all), cosine, signed_sine, matrix)
    k_rot = lax.optimization_barrier(k_rot.astype(jnp.bfloat16))
    tile_shape = (TILES, TILE_TOK, head_count, HEAD_DIM)
    q_tiles = q_rot.reshape(tile_shape)
    k_tiles = k_rot.reshape(tile_shape)
    v_tiles = values_in.reshape(tile_shape)
    g_tiles = grad_out.reshape(tile_shape)

    def near_of(tile_at):
        row_of = tile_at // GRID_COLS
        col_of = tile_at % GRID_COLS
        starts = []
        flag_list = []
        for row_step in (-1, 0, 1):
            for col_step in (-1, 0, 1):
                starts.append(jnp.clip(tile_at + row_step * GRID_COLS + col_step, 0, TILES - 1).astype(jnp.int32))
                near_flag = (row_of + row_step >= 0) & (row_of + row_step < GRID_ROWS) & (col_of + col_step >= 0) & (col_of + col_step < GRID_COLS)
                flag_list.append(jnp.broadcast_to(near_flag, (TILE_TOK,)))
        return starts, jnp.concatenate(flag_list)

    def gather_near(tile_stack, starts, axis_dim):
        return jnp.concatenate([lax.dynamic_index_in_dim(tile_stack, start_at, 0, keepdims=False) for start_at in starts], axis=axis_dim)

    def query_pass(tile_at):
        starts, usable = near_of(tile_at)
        q_tile = lax.dynamic_index_in_dim(q_tiles, tile_at, 0, keepdims=False)
        g_tile = lax.dynamic_index_in_dim(g_tiles, tile_at, 0, keepdims=False)
        return query_kernel(q_tile, g_tile, gather_near(k_tiles, starts, 0), gather_near(v_tiles, starts, 0), usable)

    attended, log_norm, row_dots, dq_rot = lax.map(query_pass, jnp.arange(TILES, dtype=jnp.int32))

    def key_pass(tile_at):
        starts, usable = near_of(tile_at)
        k_tile = lax.dynamic_index_in_dim(k_tiles, tile_at, 0, keepdims=False)
        v_tile = lax.dynamic_index_in_dim(v_tiles, tile_at, 0, keepdims=False)
        return key_kernel(k_tile, v_tile, gather_near(q_tiles, starts, 0), gather_near(g_tiles, starts, 0), gather_near(log_norm, starts, 1), gather_near(row_dots, starts, 1), usable)

    dk_rot, dv_sum = lax.map(key_pass, jnp.arange(TILES, dtype=jnp.int32))
    query_grad = turn_back(dq_rot.reshape(shape_all), cosine, signed_sine, matrix).astype(jnp.bfloat16).reshape(TOKENS, -1)
    key_grad = turn_back(dk_rot.reshape(shape_all), cosine, signed_sine, matrix).astype(jnp.bfloat16).reshape(TOKENS, -1)
    value_grad = dv_sum.reshape(TOKENS, -1).astype(jnp.bfloat16)
    return attended.reshape(TOKENS, -1), query_grad, key_grad, value_grad
```

```python
import functools
import math

import jax
import jax.numpy as jnp
from jax import lax
from jax.experimental import pallas as pl
from jax.experimental.pallas import tpu as pltpu
from jax.sharding import PartitionSpec as P

HEAD_DIM = 128
TILE_TOK = 256
GRID_COLS = 8
ROW_TOK = TILE_TOK * GRID_COLS
HALF_TOK = ROW_TOK // 2
BAND_TOK = HALF_TOK + TILE_TOK
THETA = 10000.0
MESH = pl.DeviceIdType.MESH
INV_ROOT = HEAD_DIM ** (-0.5)
VMEM_LIMIT = 56 * 1024 * 1024


def angle_tables(row_ids, col_ids):
    turned = 7 * HEAD_DIM // 16
    unturned = HEAD_DIM - 2 * turned
    slot_ids = lax.iota(jnp.int32, HEAD_DIM)
    offset = slot_ids - unturned
    by_column = offset >= turned
    within = jnp.where(by_column, offset - turned, offset)
    paired = jnp.maximum(within, 0) // 2
    frequency = jnp.exp(paired.astype(jnp.float32) * (-2.0 * math.log(THETA) / turned))
    chosen = jnp.where(by_column[None, :], col_ids[:, None], row_ids[:, None]).astype(jnp.float32)
    angles = chosen * frequency[None, :]
    active = (offset >= 0)[None, :]
    cosine = jnp.where(active, jnp.cos(angles), 1.0)
    parity = jnp.where(within % 2 == 0, -1.0, 1.0)
    signed_sine = jnp.where(active, jnp.sin(angles) * parity[None, :], 0.0)
    return (cosine, signed_sine)


def swapped(x):
    lane = lax.broadcasted_iota(jnp.int32, x.shape, 1)
    after = pltpu.roll(x, HEAD_DIM - 1, 1)
    before = pltpu.roll(x, 1, 1)
    return jnp.where(lane % 2 == 0, after, before)


def pack_kernel(q_ref, k_ref, v_ref, g_ref, cos_ref, sin_ref, packed):
    cosine, sine = cos_ref[...], sin_ref[...]
    for head in range(packed.shape[0]):
        cols = slice(head * HEAD_DIM, (head + 1) * HEAD_DIM)
        for slot, ref in ((0, k_ref), (2, q_ref)):
            x = ref[:, cols].astype(jnp.float32)
            packed[head, slot] = (x * cosine + swapped(x) * sine).astype(jnp.bfloat16)
        packed[head, 1] = v_ref[:, cols]
        packed[head, 3] = g_ref[:, cols]


def unpack_kernel(flag_ref, out_ref, halo_ref, cos_ref, sin_ref, att_ref, dq_ref, dk_ref, dv_ref):
    cosine, sine = cos_ref[...], sin_ref[...]
    heads, _, length, _ = out_ref.shape
    halo_heads, _, piece, _ = halo_ref.shape

    def back(x):
        return (x * cosine + swapped(x * sine)).astype(jnp.bfloat16)

    for head in range(heads):
        cols = slice(head * HEAD_DIM, (head + 1) * HEAD_DIM)
        att_ref[:, cols] = out_ref[head, 2]
        dq_ref[:, cols] = back(out_ref[head, 3].astype(jnp.float32))
        pair = [out_ref[head, i].astype(jnp.float32) for i in range(2)]
        at = head - (heads - halo_heads)
        if at >= 0:
            for i in range(2):
                extra = halo_ref[at, i].astype(jnp.float32)
                first = jnp.where(flag_ref[0] > 0, extra, 0.0)
                last = jnp.where(flag_ref[1] > 0, extra, 0.0)
                if piece == length:
                    pair[i] = pair[i] + first + last
                else:
                    gap = jnp.zeros((length - piece, HEAD_DIM), jnp.float32)
                    pair[i] = (
                        pair[i]
                        + jnp.concatenate([first, gap], axis=0)
                        + jnp.concatenate([gap, last], axis=0)
                    )
        dk_ref[:, cols] = back(pair[0])
        dv_ref[:, cols] = pair[1].astype(jnp.bfloat16)


class Place:
    def __init__(self, head_axis, length):
        self.tile = lax.axis_index("tile")
        self.head = lax.axis_index("head")
        self.heads = head_axis
        self.length = length
        self.piece = min(length, TILE_TOK)
        self.pieces = TILE_TOK // self.piece
        self.plane = self.tile // 4
        self.x = (self.tile // 2) % 2
        self.core = self.tile % 2
        self.pos = self.core * head_axis + self.head
        self.worker = self.x * head_axis + self.head
        self.row = 2 * self.plane + self.core
        self.rows = lax.axis_size("tile") // 2
        self.has_up = self.row > 0
        self.has_down = self.row < self.rows - 1
        self.tile_up = self.tile - 3 + 2 * self.core
        self.tile_down = self.tile + 1 + 2 * self.core

    def worker_at(self, step):
        worker = (self.worker + step) % (2 * self.heads)
        x, head = worker // self.heads, worker % self.heads
        tile = self.plane * 4 + x * 2 + self.x
        here = (tile == self.tile) & (head == self.head)
        return worker, (tile, head), here

    def owner_at(self, step):
        pos = (self.pos + step) % (2 * self.heads)
        core, head = pos // self.heads, pos % self.heads
        tile = self.plane * 4 + self.core * 2 + core
        here = (tile == self.tile) & (head == self.head)
        return pos, core, head, (tile, head), here

    def lends(self, core, head):
        return jnp.where(core == 1, head, self.heads - 1 - head) < self.pieces

    def lent_from(self, core):
        return pl.multiple_of((1 - core) * (self.length - self.piece), self.piece)

    def lent_to(self, core, head):
        low = (head - (self.heads - self.pieces)) * self.piece
        high = HALF_TOK + head * self.piece
        return pl.multiple_of(core * high + (1 - core) * low, self.piece)

    def span(self, start, size=None):
        size = self.length if size is None else size
        return pl.ds(pl.multiple_of(start, self.piece), size)


def move(src, dst, send_sem, recv_sem, device, here):
    remote = pltpu.make_async_remote_copy(
        src_ref=src,
        dst_ref=dst,
        send_sem=send_sem,
        recv_sem=recv_sem,
        device_id=device,
        device_id_type=MESH,
    )

    @pl.when(here)
    def _():
        pltpu.make_async_copy(src, dst, recv_sem).start()

    @pl.when(jnp.logical_not(here))
    def _():
        remote.start()

    return remote


def wait_in(dst, sem):
    pltpu.make_async_copy(dst, dst, sem).wait()


def unless(flag):
    return pl.when(jnp.logical_not(flag))


def greet(place, devices):
    barrier = pltpu.get_barrier_semaphore()

    def tell(device):
        pl.semaphore_signal(barrier, inc=1, device_id=device, device_id_type=MESH)

    for device, here in devices:
        @unless(here)
        def _():
            tell(device)

    @pl.when(place.has_up)
    def _():
        tell((place.tile_up, place.head))

    @pl.when(place.has_down)
    def _():
        tell((place.tile_down, place.head))

    own = (place.x == place.core).astype(jnp.int32)
    ends = place.has_up.astype(jnp.int32) + place.has_down.astype(jnp.int32)
    pl.semaphore_wait(barrier, len(devices) - own + ends)


def gather_kernel(
    head_axis, length, packed, kva, kvb, qga, qgb, send, recv, row_send, row_recv, row_send_b, row_recv_b
):
    place = Place(head_axis, length)
    steps = 2 * head_axis
    greet(place, [place.owner_at(s)[3:5] for s in range(steps)])
    first_b = 2 * head_axis
    sent = []

    def kv_copies(step):
        worker, device, here = place.worker_at(step)
        mine = place.span(place.pos * length)
        head_b = first_b + worker // 2
        side = worker % 2
        copy = move(
            packed.at[worker, pl.ds(0, 2)],
            kva.at[1, :, mine],
            send.at[0, step],
            recv.at[0, place.pos],
            device,
            here,
        )
        sent.append((copy, jnp.logical_not(here)))
        whole = side == place.core
        lent = jnp.logical_not(whole) & place.lends(place.core, place.head)

        @pl.when(whole)
        def _():
            move(
                packed.at[head_b, pl.ds(0, 2)],
                kvb.at[1, :, place.span(place.core * TILE_TOK + place.head * length)],
                send.at[1, step],
                recv.at[1, place.pos],
                device,
                here,
            )

        @pl.when(lent)
        def _():
            move(
                packed.at[head_b, pl.ds(0, 2), pl.ds(place.lent_from(place.core), place.piece)],
                kvb.at[1, :, pl.ds(place.lent_to(place.core, place.head), place.piece)],
                send.at[1, step],
                recv.at[1, place.pos],
                device,
                here,
            )

        return whole, lent

    def qg_copies(step):
        worker, device, here = place.worker_at(step)
        mine = place.span(place.pos * length)
        move(
            packed.at[worker, pl.ds(2, 2)],
            qga.at[:, mine],
            send.at[2, step],
            recv.at[2, place.pos],
            device,
            here,
        )

        @pl.when(worker % 2 == place.core)
        def _():
            move(
                packed.at[first_b + worker // 2, pl.ds(2, 2)],
                qgb.at[:, place.span(place.head * length)],
                send.at[3, step],
                recv.at[3, place.pos],
                device,
                here,
            )

    for step in range(steps):
        kv_copies(step)
    for step in range(steps):
        qg_copies(step)

    side = place.worker % 2

    def pass_on(ref, part, sems_out, sems_in):
        own = ref.at[1] if part is None else ref.at[1, :, part]
        for way, (exists, tile, slot) in enumerate(
            ((place.has_down, place.tile_down, 0), (place.has_up, place.tile_up, 2))
        ):
            there = ref.at[slot] if part is None else ref.at[slot, :, part]
            other = ref.at[2 - slot] if part is None else ref.at[2 - slot, :, part]

            @pl.when(exists)
            def _():
                pltpu.make_async_remote_copy(
                    src_ref=own,
                    dst_ref=there,
                    send_sem=sems_out(way),
                    recv_sem=sems_in(way),
                    device_id=(tile, place.head),
                    device_id_type=MESH,
                ).start()

            @unless(exists)
            def _():
                pltpu.make_async_copy(own, other, sems_in(1 - way)).start()

    for step in range(steps):
        pos, core, head, _, _ = place.owner_at(step)
        part = place.span(pos * length)
        wait_in(kva.at[1, :, part], recv.at[0, pos])
        pass_on(
            kva,
            part,
            lambda way: row_send.at[way, pos],
            lambda way: row_recv.at[way, pos],
        )
    for step in range(steps):
        pos, core, head, _, _ = place.owner_at(step)

        @pl.when(core == side)
        def _():
            wait_in(kvb.at[1, :, place.span(core * TILE_TOK + head * length)], recv.at[1, pos])

        @pl.when((core != side) & place.lends(core, head))
        def _():
            wait_in(kvb.at[1, :, pl.ds(place.lent_to(core, head), place.piece)], recv.at[1, pos])

    pass_on(kvb, None, lambda way: row_send_b.at[way], lambda way: row_recv_b.at[way])

    for step in range(steps):
        pos, core, head, _, _ = place.owner_at(step)
        wait_in(qga.at[:, place.span(pos * length)], recv.at[2, pos])

        @pl.when(core == side)
        def _():
            wait_in(qgb.at[:, place.span(head * length)], recv.at[3, pos])

    for way, slot in enumerate((0, 2)):
        for step in range(steps):
            pos = place.owner_at(step)[0]
            wait_in(kva.at[slot, :, place.span(pos * length)], row_recv.at[way, pos])
        wait_in(kvb.at[slot], row_recv_b.at[way])

        exists = (place.has_down, place.has_up)[way]

        @pl.when(exists)
        def _():
            for step in range(steps):
                pos = place.owner_at(step)[0]
                wait_in(kva.at[1, :, place.span(pos * length)], row_send.at[way, pos])
            wait_in(kvb.at[1], row_send_b.at[way])

    for step in range(steps):
        worker, device, here = place.worker_at(step)
        whole = worker % 2 == place.core
        lent = jnp.logical_not(whole) & place.lends(place.core, place.head)
        head_b = first_b + worker // 2

        @unless(here)
        def _():
            wait_in(packed.at[worker, pl.ds(0, 2)], send.at[0, step])
            wait_in(packed.at[worker, pl.ds(2, 2)], send.at[2, step])

            @pl.when(whole)
            def _():
                wait_in(packed.at[head_b, pl.ds(0, 2)], send.at[1, step])
                wait_in(packed.at[head_b, pl.ds(2, 2)], send.at[3, step])

            @pl.when(lent)
            def _():
                wait_in(
                    packed.at[head_b, pl.ds(0, 2), pl.ds(place.lent_from(place.core), place.piece)],
                    send.at[1, step],
                )


def scatter_kernel(
    head_axis,
    length,
    own_a,
    own_b,
    far_a,
    far_b,
    aqa,
    aqb,
    out,
    halo,
    got_a,
    got_b,
    sum_a,
    sum_b,
    send,
    recv,
    row_send,
    row_recv,
):
    place = Place(head_axis, length)
    steps = 2 * head_axis
    greet(place, [place.worker_at(s)[1:3] for s in range(steps)])
    first_b = 2 * head_axis
    side = place.worker % 2
    head_b = first_b + place.worker // 2

    rows = ((place.has_up, place.tile_up), (place.has_down, place.tile_down))
    for way, (exists, tile) in enumerate(rows):
        for kind, (far, got) in enumerate(((far_a, got_a), (far_b, got_b))):
            @pl.when(exists)
            def _():
                pltpu.make_async_remote_copy(
                    src_ref=far.at[way],
                    dst_ref=got.at[way],
                    send_sem=row_send.at[way, kind],
                    recv_sem=row_recv.at[way, kind],
                    device_id=(tile, place.head),
                    device_id_type=MESH,
                ).start()

            @unless(exists)
            def _():
                pltpu.make_async_copy(
                    far.at[way], got.at[1 - way], row_recv.at[1 - way, kind]
                ).start()

    for step in range(steps):
        pos, core, head, device, here = place.owner_at(step)
        move(
            aqa.at[:, place.span(pos * length)],
            out.at[place.worker, pl.ds(2, 2)],
            send.at[0, step],
            recv.at[0, place.worker],
            device,
            here,
        )

        @pl.when(core == side)
        def _():
            move(
                aqb.at[:, place.span(head * length)],
                out.at[head_b, pl.ds(2, 2)],
                send.at[1, step],
                recv.at[1, place.worker],
                device,
                here,
            )

    for way in range(2):
        for kind, got in enumerate((got_a, got_b)):
            wait_in(got.at[way], row_recv.at[way, kind])

    for own, got, total in ((own_a, got_a, sum_a), (own_b, got_b, sum_b)):
        chunk = TILE_TOK

        def add(i, carry, own=own, got=got, total=total):
            at = pl.ds(pl.multiple_of(i * chunk, chunk), chunk)
            for j in range(2):
                total[j, at] = (
                    own[j, at]
                    + got[0, j, at].astype(jnp.float32)
                    + got[1, j, at].astype(jnp.float32)
                ).astype(jnp.bfloat16)
            return carry

        lax.fori_loop(0, own.shape[1] // chunk, add, 0)

    for step in range(steps):
        pos, core, head, device, here = place.owner_at(step)
        move(
            sum_a.at[:, place.span(pos * length)],
            out.at[place.worker, pl.ds(0, 2)],
            send.at[2, step],
            recv.at[2, place.worker],
            device,
            here,
        )

        @pl.when(core == side)
        def _():
            move(
                sum_b.at[:, place.span(core * TILE_TOK + head * length)],
                out.at[head_b, pl.ds(0, 2)],
                send.at[3, step],
                recv.at[3, place.worker],
                device,
                here,
            )

        @pl.when((core != side) & place.lends(core, head))
        def _():
            move(
                sum_b.at[:, pl.ds(place.lent_to(core, head), place.piece)],
                halo.at[place.worker // 2],
                send.at[3, step],
                recv.at[3, place.worker],
                device,
                here,
            )

    for way, (exists, tile) in enumerate(rows):
        @pl.when(exists)
        def _():
            for kind, far in enumerate((far_a, far_b)):
                wait_in(far.at[way], row_send.at[way, kind])

    for step in range(steps):
        pos, core, head, device, here = place.owner_at(step)
        part = place.span(pos * length)

        @unless(here)
        def _():
            wait_in(aqa.at[:, part], send.at[0, step])
            wait_in(sum_a.at[:, part], send.at[2, step])

            @pl.when(core == side)
            def _():
                wait_in(aqb.at[:, place.span(head * length)], send.at[1, step])
                wait_in(
                    sum_b.at[:, place.span(core * TILE_TOK + head * length)], send.at[3, step]
                )

            @pl.when((core != side) & place.lends(core, head))
            def _():
                wait_in(
                    sum_b.at[:, pl.ds(place.lent_to(core, head), place.piece)], send.at[3, step]
                )

    for step in range(steps):
        worker, _, _ = place.worker_at(step)
        wait_in(out.at[worker, pl.ds(2, 2)], recv.at[0, worker])
        wait_in(out.at[worker, pl.ds(0, 2)], recv.at[2, worker])
        whole = worker % 2 == place.core
        lent = jnp.logical_not(whole) & place.lends(place.core, place.head)

        @pl.when(whole)
        def _():
            wait_in(out.at[first_b + worker // 2, pl.ds(2, 2)], recv.at[1, worker])
            wait_in(out.at[first_b + worker // 2, pl.ds(0, 2)], recv.at[3, worker])

        @pl.when(lent)
        def _():
            wait_in(halo.at[worker // 2], recv.at[3, worker])


BIG = 1e30


def attend_kernel(
    flags, kva, kvb, qga, qgb, aqa, aqb, own_a, own_b, far_a, far_b, trans_a, trans_b, acc_a, acc_b, probs
):
    side = flags[2]
    to_log2 = INV_ROOT / math.log(2.0)
    f32 = jnp.float32
    row_ok = (flags[0] > 0, True, flags[1] > 0)

    for kv, trans, acc in ((kva, trans_a, acc_a), (kvb, trans_b, acc_b)):
        acc[...] = jnp.zeros_like(acc)

        def turn(i, carry, kv=kv, trans=trans):
            at = pl.ds(pl.multiple_of(i * TILE_TOK, TILE_TOK), TILE_TOK)
            for dr in range(3):
                for j in range(2):
                    trans[dr, j, :, at] = kv[dr, j, at].T
            return carry

        lax.fori_loop(0, kv.shape[2] // TILE_TOK, turn, 0)

    def unit(i, col, base, kv, qg, aq, trans, acc):
        band = kv.shape[2] // TILE_TOK
        start = jnp.clip(col - 1 - base, 0, band - 3)
        here = pl.ds(pl.multiple_of(i * TILE_TOK, TILE_TOK), TILE_TOK)
        q, g = qg[0, here], qg[1, here]
        tiles = []
        for dr in range(3):
            for j in range(3):
                at = pl.ds(pl.multiple_of((start + j) * TILE_TOK, TILE_TOK), TILE_TOK)
                away = base + start + j - col
                ok = (away >= -1) & (away <= 1)
                if dr != 1:
                    ok = ok & row_ok[dr]
                tiles.append((dr, at, ok))
        over_lanes = (((1,), (1,)), ((), ()))
        top = jnp.full((1, TILE_TOK), -BIG, f32)
        for n, (dr, at, ok) in enumerate(tiles):
            s = lax.dot_general(kv[dr, 0, at], q, over_lanes, preferred_element_type=f32)
            probs[n] = s
            top = jnp.maximum(top, jnp.where(ok, jnp.max(s, axis=0, keepdims=True), -BIG))
        top = top * to_log2
        total = jnp.zeros((1, TILE_TOK), f32)
        att = jnp.zeros((HEAD_DIM, TILE_TOK), f32)
        for n, (dr, at, ok) in enumerate(tiles):
            p = jnp.exp2(probs[n] * to_log2 - jnp.where(ok, top, BIG))
            probs[n] = p
            total = total + jnp.sum(p, axis=0, keepdims=True)
            att = att + jnp.dot(
                trans[dr, 1, :, at], p.astype(jnp.bfloat16), preferred_element_type=f32
            )
        inverse = 1.0 / total
        att = (att * inverse).astype(jnp.bfloat16)
        aq[0, here] = att.T
        dots = jnp.sum(att.astype(f32) * g.T.astype(f32), axis=0, keepdims=True)
        dq = jnp.zeros((HEAD_DIM, TILE_TOK), f32)
        for n, (dr, at, ok) in enumerate(tiles):
            w = probs[n] * inverse
            dp = lax.dot_general(kv[dr, 1, at], g, over_lanes, preferred_element_type=f32)
            ds = (w * (dp - dots)).astype(jnp.bfloat16)
            acc[dr, 1, at] += jnp.dot(w.astype(jnp.bfloat16), g, preferred_element_type=f32)
            acc[dr, 0, at] += jnp.dot(ds, q, preferred_element_type=f32)
            dq = dq + jnp.dot(trans[dr, 0, :, at], ds, preferred_element_type=f32)
        aq[1, here] = (dq * INV_ROOT).T.astype(jnp.bfloat16)

    def unit_a(i, carry):
        unit(i, i, 0, kva, qga, aqa, trans_a, acc_a)
        return carry

    def unit_b(i, carry):
        unit(i, i + side * (GRID_COLS // 2), side * (GRID_COLS // 2 - 1), kvb, qgb, aqb, trans_b, acc_b)
        return carry

    lax.fori_loop(0, GRID_COLS, unit_a, 0)
    lax.fori_loop(0, GRID_COLS // 2, unit_b, 0)
    for acc, own, far in ((acc_a, own_a, far_a), (acc_b, own_b, far_b)):
        for j, scale in enumerate((INV_ROOT, 1.0)):
            own[j] = acc[1, j] * scale
            far[0, j] = (acc[0, j] * scale).astype(jnp.bfloat16)
            far[1, j] = (acc[2, j] * scale).astype(jnp.bfloat16)


def local(head_axis, queries, keys_in, values_in, grad_out, positions):
    length, width = queries.shape
    heads = width // HEAD_DIM
    bf16, f32 = jnp.bfloat16, jnp.float32
    assert heads == 3 * head_axis and 2 * head_axis * length == ROW_TOK and head_axis % 2 == 0
    place = Place(head_axis, length)
    piece = place.piece
    steps = 2 * head_axis
    cosine, sine = angle_tables(positions[0], positions[1])
    any_space = pl.BlockSpec(memory_space=pl.ANY)
    vmem = pl.BlockSpec(memory_space=pltpu.VMEM)
    smem = pl.BlockSpec(memory_space=pltpu.SMEM)
    shape = jax.ShapeDtypeStruct
    dma = pltpu.SemaphoreType.DMA

    packed = pl.pallas_call(
        pack_kernel,
        out_shape=shape((heads, 4, length, HEAD_DIM), bf16),
        in_specs=[vmem] * 6,
        out_specs=vmem,
        compiler_params=pltpu.CompilerParams(vmem_limit_bytes=VMEM_LIMIT),
    )(queries, keys_in, values_in, grad_out, cosine, sine)

    kva, kvb, qga, qgb = pl.pallas_call(
        functools.partial(gather_kernel, head_axis, length),
        out_shape=(
            shape((3, 2, ROW_TOK, HEAD_DIM), bf16),
            shape((3, 2, BAND_TOK, HEAD_DIM), bf16),
            shape((2, ROW_TOK, HEAD_DIM), bf16),
            shape((2, HALF_TOK, HEAD_DIM), bf16),
        ),
        in_specs=[any_space],
        out_specs=[any_space] * 4,
        scratch_shapes=[
            dma((4, steps)),
            dma((4, steps)),
            dma((2, steps)),
            dma((2, steps)),
            dma((2,)),
            dma((2,)),
        ],
        compiler_params=pltpu.CompilerParams(collective_id=0, has_side_effects=True),
    )(packed)

    flags = jnp.stack(
        [place.has_up.astype(jnp.int32), place.has_down.astype(jnp.int32), place.worker % 2]
    ).astype(jnp.int32)
    aqa, aqb, own_a, own_b, far_a, far_b = pl.pallas_call(
        attend_kernel,
        out_shape=(
            shape((2, ROW_TOK, HEAD_DIM), bf16),
            shape((2, HALF_TOK, HEAD_DIM), bf16),
            shape((2, ROW_TOK, HEAD_DIM), f32),
            shape((2, BAND_TOK, HEAD_DIM), f32),
            shape((2, 2, ROW_TOK, HEAD_DIM), bf16),
            shape((2, 2, BAND_TOK, HEAD_DIM), bf16),
        ),
        in_specs=[smem] + [vmem] * 4,
        out_specs=[vmem] * 6,
        scratch_shapes=[
            pltpu.VMEM((3, 2, HEAD_DIM, ROW_TOK), bf16),
            pltpu.VMEM((3, 2, HEAD_DIM, BAND_TOK), bf16),
            pltpu.VMEM((3, 2, ROW_TOK, HEAD_DIM), f32),
            pltpu.VMEM((3, 2, BAND_TOK, HEAD_DIM), f32),
            pltpu.VMEM((9, TILE_TOK, TILE_TOK), f32),
        ],
        compiler_params=pltpu.CompilerParams(vmem_limit_bytes=VMEM_LIMIT),
    )(flags, kva, kvb, qga, qgb)

    out, halo = pl.pallas_call(
        functools.partial(scatter_kernel, head_axis, length),
        out_shape=(
            shape((heads, 4, length, HEAD_DIM), bf16),
            shape((head_axis, 2, piece, HEAD_DIM), bf16),
        ),
        in_specs=[vmem] * 2 + [any_space] * 4,
        out_specs=[any_space] * 2,
        scratch_shapes=[
            pltpu.VMEM((2, 2, ROW_TOK, HEAD_DIM), bf16),
            pltpu.VMEM((2, 2, BAND_TOK, HEAD_DIM), bf16),
            pltpu.VMEM((2, ROW_TOK, HEAD_DIM), bf16),
            pltpu.VMEM((2, BAND_TOK, HEAD_DIM), bf16),
            dma((4, steps)),
            dma((4, steps)),
            dma((2, 2)),
            dma((2, 2)),
        ],
        compiler_params=pltpu.CompilerParams(
            collective_id=1, has_side_effects=True, vmem_limit_bytes=VMEM_LIMIT
        ),
    )(own_a, own_b, far_a, far_b, aqa, aqb)

    lends = place.lends(place.core, place.head)
    halo_flags = jnp.stack([lends & (place.core == 1), lends & (place.core == 0)]).astype(jnp.int32)
    return pl.pallas_call(
        unpack_kernel,
        out_shape=(shape((length, width), bf16),) * 4,
        in_specs=[smem] + [vmem] * 4,
        out_specs=[vmem] * 4,
        compiler_params=pltpu.CompilerParams(vmem_limit_bytes=VMEM_LIMIT),
    )(halo_flags, out, halo, cosine, sine)


def solution(mesh):
    tokens = P(("tile", "head"), None)
    return jax.shard_map(
        functools.partial(local, mesh.shape["head"]),
        mesh=mesh,
        in_specs=(tokens, tokens, tokens, tokens, P(None, ("tile", "head"))),
        out_specs=(tokens, tokens, tokens, tokens),
        check_vma=False,
    )
```

```python
import functools
import math

import jax
import jax.numpy as jnp
from jax import lax
from jax.experimental import pallas as pl
from jax.experimental.pallas import tpu as pltpu
from jax.sharding import PartitionSpec as P

HEAD_DIM = 128
TILE_TOK = 256
GRID_COLS = 8
ROW_TOK = TILE_TOK * GRID_COLS
HALF_TOK = ROW_TOK // 2
BAND_TOK = HALF_TOK + TILE_TOK
WINDOW = 3 * TILE_TOK
THETA = 10000.0
MESH = pl.DeviceIdType.MESH
INV_ROOT = HEAD_DIM ** (-0.5)
VMEM_LIMIT = 56 * 1024 * 1024


def angle_tables(row_ids, col_ids):
    turned = 7 * HEAD_DIM // 16
    unturned = HEAD_DIM - 2 * turned
    slot_ids = lax.iota(jnp.int32, HEAD_DIM)
    offset = slot_ids - unturned
    by_column = offset >= turned
    within = jnp.where(by_column, offset - turned, offset)
    paired = jnp.maximum(within, 0) // 2
    frequency = jnp.exp(paired.astype(jnp.float32) * (-2.0 * math.log(THETA) / turned))
    chosen = jnp.where(by_column[None, :], col_ids[:, None], row_ids[:, None]).astype(jnp.float32)
    angles = chosen * frequency[None, :]
    active = (offset >= 0)[None, :]
    cosine = jnp.where(active, jnp.cos(angles), 1.0)
    parity = jnp.where(within % 2 == 0, -1.0, 1.0)
    signed_sine = jnp.where(active, jnp.sin(angles) * parity[None, :], 0.0)
    return (cosine, signed_sine)


def swapped(x):
    lane = lax.broadcasted_iota(jnp.int32, x.shape, 1)
    after = pltpu.roll(x, HEAD_DIM - 1, 1)
    before = pltpu.roll(x, 1, 1)
    return jnp.where(lane % 2 == 0, after, before)


def pack_kernel(q_ref, k_ref, v_ref, g_ref, cos_ref, sin_ref, packed):
    cosine, sine = cos_ref[...], sin_ref[...]
    for head in range(packed.shape[0]):
        cols = slice(head * HEAD_DIM, (head + 1) * HEAD_DIM)
        for slot, ref in ((0, k_ref), (2, q_ref)):
            x = ref[:, cols].astype(jnp.float32)
            packed[head, slot] = (x * cosine + swapped(x) * sine).astype(jnp.bfloat16)
        packed[head, 1] = v_ref[:, cols]
        packed[head, 3] = g_ref[:, cols]


def unpack_kernel(flag_ref, out_ref, halo_ref, cos_ref, sin_ref, att_ref, dq_ref, dk_ref, dv_ref):
    cosine, sine = cos_ref[...], sin_ref[...]
    heads, _, length, _ = out_ref.shape
    halo_heads, _, piece, _ = halo_ref.shape

    def back(x):
        return (x * cosine + swapped(x * sine)).astype(jnp.bfloat16)

    for head in range(heads):
        cols = slice(head * HEAD_DIM, (head + 1) * HEAD_DIM)
        att_ref[:, cols] = out_ref[head, 2]
        dq_ref[:, cols] = back(out_ref[head, 3].astype(jnp.float32))
        pair = [out_ref[head, i].astype(jnp.float32) for i in range(2)]
        at = head - (heads - halo_heads)
        if at >= 0:
            for i in range(2):
                extra = halo_ref[at, i].astype(jnp.float32)
                first = jnp.where(flag_ref[0] > 0, extra, 0.0)
                last = jnp.where(flag_ref[1] > 0, extra, 0.0)
                if piece == length:
                    pair[i] = pair[i] + first + last
                else:
                    gap = jnp.zeros((length - piece, HEAD_DIM), jnp.float32)
                    pair[i] = (
                        pair[i]
                        + jnp.concatenate([first, gap], axis=0)
                        + jnp.concatenate([gap, last], axis=0)
                    )
        dk_ref[:, cols] = back(pair[0])
        dv_ref[:, cols] = pair[1].astype(jnp.bfloat16)


class Place:
    def __init__(self, head_axis, length):
        self.tile = lax.axis_index("tile")
        self.head = lax.axis_index("head")
        self.heads = head_axis
        self.length = length
        self.piece = min(length, TILE_TOK)
        self.pieces = TILE_TOK // self.piece
        self.plane = self.tile // 4
        self.x = (self.tile // 2) % 2
        self.core = self.tile % 2
        self.pos = self.core * head_axis + self.head
        self.worker = self.x * head_axis + self.head
        self.row = 2 * self.plane + self.core
        self.rows = lax.axis_size("tile") // 2
        self.has_up = self.row > 0
        self.has_down = self.row < self.rows - 1
        self.tile_up = self.tile - 3 + 2 * self.core
        self.tile_down = self.tile + 1 + 2 * self.core

    def worker_at(self, step):
        worker = (self.worker + step) % (2 * self.heads)
        x, head = worker // self.heads, worker % self.heads
        tile = self.plane * 4 + x * 2 + self.x
        here = (tile == self.tile) & (head == self.head)
        return worker, (tile, head), here

    def owner_at(self, step):
        pos = (self.pos + step) % (2 * self.heads)
        core, head = pos // self.heads, pos % self.heads
        tile = self.plane * 4 + self.core * 2 + core
        here = (tile == self.tile) & (head == self.head)
        return pos, core, head, (tile, head), here

    def lends(self, core, head):
        return jnp.where(core == 1, head, self.heads - 1 - head) < self.pieces

    def lent_from(self, core):
        return pl.multiple_of((1 - core) * (self.length - self.piece), self.piece)

    def lent_to(self, core, head):
        low = (head - (self.heads - self.pieces)) * self.piece
        high = HALF_TOK + head * self.piece
        return pl.multiple_of(core * high + (1 - core) * low, self.piece)

    def span(self, start, size=None):
        size = self.length if size is None else size
        return pl.ds(pl.multiple_of(start, self.piece), size)


def move(src, dst, send_sem, recv_sem, device, here):
    remote = pltpu.make_async_remote_copy(
        src_ref=src,
        dst_ref=dst,
        send_sem=send_sem,
        recv_sem=recv_sem,
        device_id=device,
        device_id_type=MESH,
    )

    @pl.when(here)
    def _():
        pltpu.make_async_copy(src, dst, recv_sem).start()

    @pl.when(jnp.logical_not(here))
    def _():
        remote.start()

    return remote


def wait_in(dst, sem):
    pltpu.make_async_copy(dst, dst, sem).wait()


def unless(flag):
    return pl.when(jnp.logical_not(flag))


def greet(place, devices):
    barrier = pltpu.get_barrier_semaphore()

    def tell(device):
        pl.semaphore_signal(barrier, inc=1, device_id=device, device_id_type=MESH)

    for device, here in devices:
        @unless(here)
        def _():
            tell(device)

    @pl.when(place.has_up)
    def _():
        tell((place.tile_up, place.head))

    @pl.when(place.has_down)
    def _():
        tell((place.tile_down, place.head))

    own = (place.x == place.core).astype(jnp.int32)
    ends = place.has_up.astype(jnp.int32) + place.has_down.astype(jnp.int32)
    pl.semaphore_wait(barrier, len(devices) - own + ends)


def gather_kernel(
    head_axis, length, packed, kva, kvb, qga, qgb, send, recv, row_send, row_recv, row_send_b, row_recv_b
):
    place = Place(head_axis, length)
    steps = 2 * head_axis
    greet(place, [place.owner_at(s)[3:5] for s in range(steps)])
    first_b = 2 * head_axis
    sent = []

    def kv_copies(step):
        worker, device, here = place.worker_at(step)
        mine = place.span(place.pos * length)
        head_b = first_b + worker // 2
        side = worker % 2
        copy = move(
            packed.at[worker, pl.ds(0, 2)],
            kva.at[1, :, mine],
            send.at[0, step],
            recv.at[0, place.pos],
            device,
            here,
        )
        sent.append((copy, jnp.logical_not(here)))
        whole = side == place.core
        lent = jnp.logical_not(whole) & place.lends(place.core, place.head)

        @pl.when(whole)
        def _():
            move(
                packed.at[head_b, pl.ds(0, 2)],
                kvb.at[1, :, place.span(place.core * TILE_TOK + place.head * length)],
                send.at[1, step],
                recv.at[1, place.pos],
                device,
                here,
            )

        @pl.when(lent)
        def _():
            move(
                packed.at[head_b, pl.ds(0, 2), pl.ds(place.lent_from(place.core), place.piece)],
                kvb.at[1, :, pl.ds(place.lent_to(place.core, place.head), place.piece)],
                send.at[1, step],
                recv.at[1, place.pos],
                device,
                here,
            )

        return whole, lent

    def qg_copies(step):
        worker, device, here = place.worker_at(step)
        mine = place.span(place.pos * length)
        move(
            packed.at[worker, pl.ds(2, 2)],
            qga.at[:, mine],
            send.at[2, step],
            recv.at[2, place.pos],
            device,
            here,
        )

        @pl.when(worker % 2 == place.core)
        def _():
            move(
                packed.at[first_b + worker // 2, pl.ds(2, 2)],
                qgb.at[:, place.span(place.head * length)],
                send.at[3, step],
                recv.at[3, place.pos],
                device,
                here,
            )

    for step in range(steps):
        kv_copies(step)
    for step in range(steps):
        qg_copies(step)

    side = place.worker % 2

    def pass_on(ref, part, sems_out, sems_in):
        own = ref.at[1] if part is None else ref.at[1, :, part]
        for way, (exists, tile, slot) in enumerate(
            ((place.has_down, place.tile_down, 0), (place.has_up, place.tile_up, 2))
        ):
            there = ref.at[slot] if part is None else ref.at[slot, :, part]

            @pl.when(exists)
            def _():
                pltpu.make_async_remote_copy(
                    src_ref=own,
                    dst_ref=there,
                    send_sem=sems_out(way),
                    recv_sem=sems_in(way),
                    device_id=(tile, place.head),
                    device_id_type=MESH,
                ).start()

    for step in range(steps):
        pos, core, head, _, _ = place.owner_at(step)
        part = place.span(pos * length)
        wait_in(kva.at[1, :, part], recv.at[0, pos])
        pass_on(
            kva,
            part,
            lambda way: row_send.at[way, pos],
            lambda way: row_recv.at[way, pos],
        )
    for step in range(steps):
        pos, core, head, _, _ = place.owner_at(step)

        @pl.when(core == side)
        def _():
            wait_in(kvb.at[1, :, place.span(core * TILE_TOK + head * length)], recv.at[1, pos])

        @pl.when((core != side) & place.lends(core, head))
        def _():
            wait_in(kvb.at[1, :, pl.ds(place.lent_to(core, head), place.piece)], recv.at[1, pos])

    pass_on(kvb, None, lambda way: row_send_b.at[way], lambda way: row_recv_b.at[way])

    for step in range(steps):
        pos, core, head, _, _ = place.owner_at(step)
        wait_in(qga.at[:, place.span(pos * length)], recv.at[2, pos])

        @pl.when(core == side)
        def _():
            wait_in(qgb.at[:, place.span(head * length)], recv.at[3, pos])

    for way, slot in enumerate((0, 2)):
        @pl.when((place.has_up, place.has_down)[way])
        def _():
            for step in range(steps):
                pos = place.owner_at(step)[0]
                wait_in(kva.at[slot, :, place.span(pos * length)], row_recv.at[way, pos])
            wait_in(kvb.at[slot], row_recv_b.at[way])

        exists = (place.has_down, place.has_up)[way]

        @pl.when(exists)
        def _():
            for step in range(steps):
                pos = place.owner_at(step)[0]
                wait_in(kva.at[1, :, place.span(pos * length)], row_send.at[way, pos])
            wait_in(kvb.at[1], row_send_b.at[way])

    for step in range(steps):
        worker, device, here = place.worker_at(step)
        whole = worker % 2 == place.core
        lent = jnp.logical_not(whole) & place.lends(place.core, place.head)
        head_b = first_b + worker // 2

        @unless(here)
        def _():
            wait_in(packed.at[worker, pl.ds(0, 2)], send.at[0, step])
            wait_in(packed.at[worker, pl.ds(2, 2)], send.at[2, step])

            @pl.when(whole)
            def _():
                wait_in(packed.at[head_b, pl.ds(0, 2)], send.at[1, step])
                wait_in(packed.at[head_b, pl.ds(2, 2)], send.at[3, step])

            @pl.when(lent)
            def _():
                wait_in(
                    packed.at[head_b, pl.ds(0, 2), pl.ds(place.lent_from(place.core), place.piece)],
                    send.at[1, step],
                )


def scatter_kernel(
    head_axis,
    length,
    own_a,
    own_b,
    far_a,
    far_b,
    aqa,
    aqb,
    out,
    halo,
    got_a,
    got_b,
    sum_a,
    sum_b,
    send,
    recv,
    row_send,
    row_recv,
):
    place = Place(head_axis, length)
    steps = 2 * head_axis
    greet(place, [place.worker_at(s)[1:3] for s in range(steps)])
    first_b = 2 * head_axis
    side = place.worker % 2
    head_b = first_b + place.worker // 2

    rows = ((place.has_up, place.tile_up), (place.has_down, place.tile_down))
    for way, (exists, tile) in enumerate(rows):
        for kind, (far, got) in enumerate(((far_a, got_a), (far_b, got_b))):
            @pl.when(exists)
            def _():
                pltpu.make_async_remote_copy(
                    src_ref=far.at[way],
                    dst_ref=got.at[way],
                    send_sem=row_send.at[way, kind],
                    recv_sem=row_recv.at[way, kind],
                    device_id=(tile, place.head),
                    device_id_type=MESH,
                ).start()

    for step in range(steps):
        pos, core, head, device, here = place.owner_at(step)
        move(
            aqa.at[:, place.span(pos * length)],
            out.at[place.worker, pl.ds(2, 2)],
            send.at[0, step],
            recv.at[0, place.worker],
            device,
            here,
        )

        @pl.when(core == side)
        def _():
            move(
                aqb.at[:, place.span(head * length)],
                out.at[head_b, pl.ds(2, 2)],
                send.at[1, step],
                recv.at[1, place.worker],
                device,
                here,
            )

    for way, exists in enumerate((place.has_down, place.has_up)):
        for kind, got in enumerate((got_a, got_b)):
            @pl.when(exists)
            def _():
                wait_in(got.at[way], row_recv.at[way, kind])

            @unless(exists)
            def _():
                got[way] = jnp.zeros(got.shape[1:], got.dtype)

    for own, got, total in ((own_a, got_a, sum_a), (own_b, got_b, sum_b)):
        chunk = TILE_TOK

        def add(i, carry, own=own, got=got, total=total):
            at = pl.ds(pl.multiple_of(i * chunk, chunk), chunk)
            for j in range(2):
                total[j, at] = (
                    own[j, at]
                    + got[0, j, at].astype(jnp.float32)
                    + got[1, j, at].astype(jnp.float32)
                ).astype(jnp.bfloat16)
            return carry

        lax.fori_loop(0, own.shape[1] // chunk, add, 0)

    for step in range(steps):
        pos, core, head, device, here = place.owner_at(step)
        move(
            sum_a.at[:, place.span(pos * length)],
            out.at[place.worker, pl.ds(0, 2)],
            send.at[2, step],
            recv.at[2, place.worker],
            device,
            here,
        )

        @pl.when(core == side)
        def _():
            move(
                sum_b.at[:, place.span(core * TILE_TOK + head * length)],
                out.at[head_b, pl.ds(0, 2)],
                send.at[3, step],
                recv.at[3, place.worker],
                device,
                here,
            )

        @pl.when((core != side) & place.lends(core, head))
        def _():
            move(
                sum_b.at[:, pl.ds(place.lent_to(core, head), place.piece)],
                halo.at[place.worker // 2],
                send.at[3, step],
                recv.at[3, place.worker],
                device,
                here,
            )

    for way, (exists, tile) in enumerate(rows):
        @pl.when(exists)
        def _():
            for kind, far in enumerate((far_a, far_b)):
                wait_in(far.at[way], row_send.at[way, kind])

    for step in range(steps):
        pos, core, head, device, here = place.owner_at(step)
        part = place.span(pos * length)

        @unless(here)
        def _():
            wait_in(aqa.at[:, part], send.at[0, step])
            wait_in(sum_a.at[:, part], send.at[2, step])

            @pl.when(core == side)
            def _():
                wait_in(aqb.at[:, place.span(head * length)], send.at[1, step])
                wait_in(
                    sum_b.at[:, place.span(core * TILE_TOK + head * length)], send.at[3, step]
                )

            @pl.when((core != side) & place.lends(core, head))
            def _():
                wait_in(
                    sum_b.at[:, pl.ds(place.lent_to(core, head), place.piece)], send.at[3, step]
                )

    for step in range(steps):
        worker, _, _ = place.worker_at(step)
        wait_in(out.at[worker, pl.ds(2, 2)], recv.at[0, worker])
        wait_in(out.at[worker, pl.ds(0, 2)], recv.at[2, worker])
        whole = worker % 2 == place.core
        lent = jnp.logical_not(whole) & place.lends(place.core, place.head)

        @pl.when(whole)
        def _():
            wait_in(out.at[first_b + worker // 2, pl.ds(2, 2)], recv.at[1, worker])
            wait_in(out.at[first_b + worker // 2, pl.ds(0, 2)], recv.at[3, worker])

        @pl.when(lent)
        def _():
            wait_in(halo.at[worker // 2], recv.at[3, worker])


BIG = 1e30


def attend_kernel(
    flags, kva, kvb, qga, qgb, aqa, aqb, own_a, own_b, far_a, far_b, trans_a, trans_b, acc_a, acc_b, probs
):
    side = flags[2]
    to_log2 = INV_ROOT / math.log(2.0)
    f32 = jnp.float32
    row_ok = (flags[0] > 0, True, flags[1] > 0)
    rows = (1 - flags[0], 1, 1 + flags[1])

    for kv, trans, acc in ((kva, trans_a, acc_a), (kvb, trans_b, acc_b)):
        acc[...] = jnp.zeros_like(acc)

        def turn(i, carry, kv=kv, trans=trans):
            at = pl.ds(pl.multiple_of(i * TILE_TOK, TILE_TOK), TILE_TOK)
            for dr in range(3):
                for j in range(2):
                    trans[dr, j, :, at] = kv[rows[dr], j, at].T
            return carry

        lax.fori_loop(0, kv.shape[2] // TILE_TOK, turn, 0)

    def unit(i, col, base, kv, qg, aq, trans, acc):
        band = kv.shape[2] // TILE_TOK
        start = jnp.clip(col - 1 - base, 0, band - 3)
        here = pl.ds(pl.multiple_of(i * TILE_TOK, TILE_TOK), TILE_TOK)
        at = pl.ds(pl.multiple_of(start * TILE_TOK, TILE_TOK), WINDOW)
        q, g = qg[0, here], qg[1, here]
        ok = []
        for dr in range(3):
            for j in range(3):
                away = base + start + j - col
                near = (away >= -1) & (away <= 1)
                ok.append(near if dr == 1 else near & row_ok[dr])
        parts = [slice(j * TILE_TOK, (j + 1) * TILE_TOK) for j in range(3)]
        over_lanes = (((1,), (1,)), ((), ()))
        top = jnp.full((1, TILE_TOK), -BIG, f32)
        for dr in range(3):
            s = lax.dot_general(kv[rows[dr], 0, at], q, over_lanes, preferred_element_type=f32)
            probs[dr] = s
            for j in range(3):
                best = jnp.max(s[parts[j]], axis=0, keepdims=True)
                top = jnp.maximum(top, jnp.where(ok[3 * dr + j], best, -BIG))
        top = top * to_log2
        total = jnp.zeros((1, TILE_TOK), f32)
        att = jnp.zeros((HEAD_DIM, TILE_TOK), f32)
        for dr in range(3):
            halves = []
            for j in range(3):
                p = jnp.exp2(probs[dr, parts[j]] * to_log2 - jnp.where(ok[3 * dr + j], top, BIG))
                probs[dr, parts[j]] = p
                total = total + jnp.sum(p, axis=0, keepdims=True)
                halves.append(p.astype(jnp.bfloat16))
            att = att + jnp.dot(
                trans[dr, 1, :, at], jnp.concatenate(halves, axis=0), preferred_element_type=f32
            )
        inverse = 1.0 / total
        att = (att * inverse).astype(jnp.bfloat16)
        aq[0, here] = att.T
        dots = jnp.sum(att.astype(f32) * g.T.astype(f32), axis=0, keepdims=True)
        dq = jnp.zeros((HEAD_DIM, TILE_TOK), f32)
        for dr in range(3):
            w = probs[dr] * inverse
            dp = lax.dot_general(kv[rows[dr], 1, at], g, over_lanes, preferred_element_type=f32)
            ds = (w * (dp - dots)).astype(jnp.bfloat16)
            acc[dr, 1, at] += jnp.dot(w.astype(jnp.bfloat16), g, preferred_element_type=f32)
            acc[dr, 0, at] += jnp.dot(ds, q, preferred_element_type=f32)
            dq = dq + jnp.dot(trans[dr, 0, :, at], ds, preferred_element_type=f32)
        aq[1, here] = (dq * INV_ROOT).T.astype(jnp.bfloat16)

    def unit_a(i, carry):
        unit(i, i, 0, kva, qga, aqa, trans_a, acc_a)
        return carry

    def unit_b(i, carry):
        unit(i, i + side * (GRID_COLS // 2), side * (GRID_COLS // 2 - 1), kvb, qgb, aqb, trans_b, acc_b)
        return carry

    lax.fori_loop(0, GRID_COLS, unit_a, 0)
    lax.fori_loop(0, GRID_COLS // 2, unit_b, 0)
    for acc, own, far in ((acc_a, own_a, far_a), (acc_b, own_b, far_b)):
        for j, scale in enumerate((INV_ROOT, 1.0)):
            own[j] = acc[1, j] * scale
            far[0, j] = (acc[0, j] * scale).astype(jnp.bfloat16)
            far[1, j] = (acc[2, j] * scale).astype(jnp.bfloat16)


def local(head_axis, queries, keys_in, values_in, grad_out, positions):
    length, width = queries.shape
    heads = width // HEAD_DIM
    bf16, f32 = jnp.bfloat16, jnp.float32
    assert heads == 3 * head_axis and 2 * head_axis * length == ROW_TOK and head_axis % 2 == 0
    place = Place(head_axis, length)
    piece = place.piece
    steps = 2 * head_axis
    cosine, sine = angle_tables(positions[0], positions[1])
    any_space = pl.BlockSpec(memory_space=pl.ANY)
    vmem = pl.BlockSpec(memory_space=pltpu.VMEM)
    smem = pl.BlockSpec(memory_space=pltpu.SMEM)
    shape = jax.ShapeDtypeStruct
    dma = pltpu.SemaphoreType.DMA

    packed = pl.pallas_call(
        pack_kernel,
        out_shape=shape((heads, 4, length, HEAD_DIM), bf16),
        in_specs=[vmem] * 6,
        out_specs=vmem,
        compiler_params=pltpu.CompilerParams(vmem_limit_bytes=VMEM_LIMIT),
    )(queries, keys_in, values_in, grad_out, cosine, sine)

    kva, kvb, qga, qgb = pl.pallas_call(
        functools.partial(gather_kernel, head_axis, length),
        out_shape=(
            shape((3, 2, ROW_TOK, HEAD_DIM), bf16),
            shape((3, 2, BAND_TOK, HEAD_DIM), bf16),
            shape((2, ROW_TOK, HEAD_DIM), bf16),
            shape((2, HALF_TOK, HEAD_DIM), bf16),
        ),
        in_specs=[any_space],
        out_specs=[any_space] * 4,
        scratch_shapes=[
            dma((4, steps)),
            dma((4, steps)),
            dma((2, steps)),
            dma((2, steps)),
            dma((2,)),
            dma((2,)),
        ],
        compiler_params=pltpu.CompilerParams(collective_id=0, has_side_effects=True),
    )(packed)

    flags = jnp.stack(
        [place.has_up.astype(jnp.int32), place.has_down.astype(jnp.int32), place.worker % 2]
    ).astype(jnp.int32)
    aqa, aqb, own_a, own_b, far_a, far_b = pl.pallas_call(
        attend_kernel,
        out_shape=(
            shape((2, ROW_TOK, HEAD_DIM), bf16),
            shape((2, HALF_TOK, HEAD_DIM), bf16),
            shape((2, ROW_TOK, HEAD_DIM), f32),
            shape((2, BAND_TOK, HEAD_DIM), f32),
            shape((2, 2, ROW_TOK, HEAD_DIM), bf16),
            shape((2, 2, BAND_TOK, HEAD_DIM), bf16),
        ),
        in_specs=[smem] + [vmem] * 4,
        out_specs=[vmem] * 6,
        scratch_shapes=[
            pltpu.VMEM((3, 2, HEAD_DIM, ROW_TOK), bf16),
            pltpu.VMEM((3, 2, HEAD_DIM, BAND_TOK), bf16),
            pltpu.VMEM((3, 2, ROW_TOK, HEAD_DIM), f32),
            pltpu.VMEM((3, 2, BAND_TOK, HEAD_DIM), f32),
            pltpu.VMEM((3, WINDOW, TILE_TOK), f32),
        ],
        compiler_params=pltpu.CompilerParams(vmem_limit_bytes=VMEM_LIMIT),
    )(flags, kva, kvb, qga, qgb)

    out, halo = pl.pallas_call(
        functools.partial(scatter_kernel, head_axis, length),
        out_shape=(
            shape((heads, 4, length, HEAD_DIM), bf16),
            shape((head_axis, 2, piece, HEAD_DIM), bf16),
        ),
        in_specs=[vmem] * 2 + [any_space] * 4,
        out_specs=[any_space] * 2,
        scratch_shapes=[
            pltpu.VMEM((2, 2, ROW_TOK, HEAD_DIM), bf16),
            pltpu.VMEM((2, 2, BAND_TOK, HEAD_DIM), bf16),
            pltpu.VMEM((2, ROW_TOK, HEAD_DIM), bf16),
            pltpu.VMEM((2, BAND_TOK, HEAD_DIM), bf16),
            dma((4, steps)),
            dma((4, steps)),
            dma((2, 2)),
            dma((2, 2)),
        ],
        compiler_params=pltpu.CompilerParams(
            collective_id=1, has_side_effects=True, vmem_limit_bytes=VMEM_LIMIT
        ),
    )(own_a, own_b, far_a, far_b, aqa, aqb)

    lends = place.lends(place.core, place.head)
    halo_flags = jnp.stack([lends & (place.core == 1), lends & (place.core == 0)]).astype(jnp.int32)
    return pl.pallas_call(
        unpack_kernel,
        out_shape=(shape((length, width), bf16),) * 4,
        in_specs=[smem] + [vmem] * 4,
        out_specs=[vmem] * 4,
        compiler_params=pltpu.CompilerParams(vmem_limit_bytes=VMEM_LIMIT),
    )(halo_flags, out, halo, cosine, sine)


def solution(mesh):
    tokens = P(("tile", "head"), None)
    return jax.shard_map(
        functools.partial(local, mesh.shape["head"]),
        mesh=mesh,
        in_specs=(tokens, tokens, tokens, tokens, P(None, ("tile", "head"))),
        out_specs=(tokens, tokens, tokens, tokens),
        check_vma=False,
    )
```

```python
import functools
import math

import jax
import jax.numpy as jnp
from jax import lax
from jax.experimental import pallas as pl
from jax.experimental.pallas import tpu as pltpu
from jax.sharding import PartitionSpec as P

HEAD_DIM = 128
TILE_TOK = 256
GRID_COLS = 8
ROW_TOK = TILE_TOK * GRID_COLS
HALF_TOK = ROW_TOK // 2
BAND_TOK = HALF_TOK + TILE_TOK
WINDOW = 3 * TILE_TOK
THETA = 10000.0
MESH = pl.DeviceIdType.MESH
INV_ROOT = HEAD_DIM ** (-0.5)
VMEM_LIMIT = 56 * 1024 * 1024


def angle_tables(row_ids, col_ids):
    turned = 7 * HEAD_DIM // 16
    unturned = HEAD_DIM - 2 * turned
    slot_ids = lax.iota(jnp.int32, HEAD_DIM)
    offset = slot_ids - unturned
    by_column = offset >= turned
    within = jnp.where(by_column, offset - turned, offset)
    paired = jnp.maximum(within, 0) // 2
    frequency = jnp.exp(paired.astype(jnp.float32) * (-2.0 * math.log(THETA) / turned))
    chosen = jnp.where(by_column[None, :], col_ids[:, None], row_ids[:, None]).astype(jnp.float32)
    angles = chosen * frequency[None, :]
    active = (offset >= 0)[None, :]
    cosine = jnp.where(active, jnp.cos(angles), 1.0)
    parity = jnp.where(within % 2 == 0, -1.0, 1.0)
    signed_sine = jnp.where(active, jnp.sin(angles) * parity[None, :], 0.0)
    return (cosine, signed_sine)


def swapped(x):
    lane = lax.broadcasted_iota(jnp.int32, x.shape, 1)
    after = pltpu.roll(x, HEAD_DIM - 1, 1)
    before = pltpu.roll(x, 1, 1)
    return jnp.where(lane % 2 == 0, after, before)


def pack_kernel(q_ref, k_ref, v_ref, g_ref, cos_ref, sin_ref, packed):
    cosine, sine = cos_ref[...], sin_ref[...]
    for head in range(packed.shape[0]):
        cols = slice(head * HEAD_DIM, (head + 1) * HEAD_DIM)
        for slot, ref in ((0, k_ref), (2, q_ref)):
            x = ref[:, cols].astype(jnp.float32)
            packed[head, slot] = (x * cosine + swapped(x) * sine).astype(jnp.bfloat16)
        packed[head, 1] = v_ref[:, cols]
        packed[head, 3] = g_ref[:, cols]


def unpack_kernel(flag_ref, out_ref, halo_ref, cos_ref, sin_ref, att_ref, dq_ref, dk_ref, dv_ref):
    cosine, sine = cos_ref[...], sin_ref[...]
    heads, _, length, _ = out_ref.shape
    halo_heads, _, piece, _ = halo_ref.shape

    def back(x):
        return (x * cosine + swapped(x * sine)).astype(jnp.bfloat16)

    for head in range(heads):
        cols = slice(head * HEAD_DIM, (head + 1) * HEAD_DIM)
        att_ref[:, cols] = out_ref[head, 2]
        dq_ref[:, cols] = back(out_ref[head, 3].astype(jnp.float32))
        pair = [out_ref[head, i].astype(jnp.float32) for i in range(2)]
        at = head - (heads - halo_heads)
        if at >= 0:
            for i in range(2):
                extra = halo_ref[at, i].astype(jnp.float32)
                first = jnp.where(flag_ref[0] > 0, extra, 0.0)
                last = jnp.where(flag_ref[1] > 0, extra, 0.0)
                if piece == length:
                    pair[i] = pair[i] + first + last
                else:
                    gap = jnp.zeros((length - piece, HEAD_DIM), jnp.float32)
                    pair[i] = (
                        pair[i]
                        + jnp.concatenate([first, gap], axis=0)
                        + jnp.concatenate([gap, last], axis=0)
                    )
        dk_ref[:, cols] = back(pair[0])
        dv_ref[:, cols] = pair[1].astype(jnp.bfloat16)


class Place:
    def __init__(self, head_axis, length):
        self.tile = lax.axis_index("tile")
        self.head = lax.axis_index("head")
        self.heads = head_axis
        self.length = length
        self.piece = min(length, TILE_TOK)
        self.pieces = TILE_TOK // self.piece
        self.plane = self.tile // 4
        self.x = (self.tile // 2) % 2
        self.core = self.tile % 2
        self.pos = self.core * head_axis + self.head
        self.worker = self.x * head_axis + self.head
        self.row = 2 * self.plane + self.core
        self.rows = lax.axis_size("tile") // 2
        self.has_up = self.row > 0
        self.has_down = self.row < self.rows - 1
        self.tile_up = self.tile - 3 + 2 * self.core
        self.tile_down = self.tile + 1 + 2 * self.core

    def worker_at(self, step):
        worker = (self.worker + step) % (2 * self.heads)
        x, head = worker // self.heads, worker % self.heads
        tile = self.plane * 4 + x * 2 + self.x
        here = (tile == self.tile) & (head == self.head)
        return worker, (tile, head), here

    def owner_at(self, step):
        pos = (self.pos + step) % (2 * self.heads)
        core, head = pos // self.heads, pos % self.heads
        tile = self.plane * 4 + self.core * 2 + core
        here = (tile == self.tile) & (head == self.head)
        return pos, core, head, (tile, head), here

    def lends(self, core, head):
        return jnp.where(core == 1, head, self.heads - 1 - head) < self.pieces

    def lent_from(self, core):
        return pl.multiple_of((1 - core) * (self.length - self.piece), self.piece)

    def lent_to(self, core, head):
        low = (head - (self.heads - self.pieces)) * self.piece
        high = HALF_TOK + head * self.piece
        return pl.multiple_of(core * high + (1 - core) * low, self.piece)

    def span(self, start, size=None):
        size = self.length if size is None else size
        return pl.ds(pl.multiple_of(start, self.piece), size)


def move(src, dst, send_sem, recv_sem, device, here):
    remote = pltpu.make_async_remote_copy(
        src_ref=src,
        dst_ref=dst,
        send_sem=send_sem,
        recv_sem=recv_sem,
        device_id=device,
        device_id_type=MESH,
    )

    @pl.when(here)
    def _():
        pltpu.make_async_copy(src, dst, recv_sem).start()

    @pl.when(jnp.logical_not(here))
    def _():
        remote.start()

    return remote


def wait_in(dst, sem):
    pltpu.make_async_copy(dst, dst, sem).wait()


def unless(flag):
    return pl.when(jnp.logical_not(flag))


def greet(place, devices):
    barrier = pltpu.get_barrier_semaphore()

    def tell(device):
        pl.semaphore_signal(barrier, inc=1, device_id=device, device_id_type=MESH)

    for device, here in devices:
        @unless(here)
        def _():
            tell(device)

    @pl.when(place.has_up)
    def _():
        tell((place.tile_up, place.head))

    @pl.when(place.has_down)
    def _():
        tell((place.tile_down, place.head))

    own = (place.x == place.core).astype(jnp.int32)
    ends = place.has_up.astype(jnp.int32) + place.has_down.astype(jnp.int32)
    pl.semaphore_wait(barrier, len(devices) - 2 * own + ends)


BIG = 1e30


def attend_kernel(
    head_axis,
    length,
    packed,
    out,
    halo,
    kva,
    kvb,
    qga,
    qgb,
    aqa,
    aqb,
    far_a,
    far_b,
    got_a,
    got_b,
    sum_a,
    sum_b,
    trans_a,
    trans_b,
    acc_a,
    acc_b,
    probs,
    send,
    recv,
    row_send,
    row_recv,
    row_send_b,
    row_recv_b,
    back_send,
    back_recv,
    ret_send,
    ret_recv,
):
    place = Place(head_axis, length)
    steps = 2 * head_axis
    first_b = 2 * head_axis
    greet(
        place,
        [place.owner_at(s)[3:5] for s in range(steps)]
        + [place.worker_at(s)[1:3] for s in range(steps)],
    )
    side = place.worker % 2
    head_b = first_b + place.worker // 2
    to_log2 = INV_ROOT / math.log(2.0)
    f32 = jnp.float32
    row_ok = (place.has_up, True, place.has_down)
    up = (place.row + place.rows - 1) // place.rows
    down = 1 - place.row // (place.rows - 1)
    rows = (1 - up, 1, 1 + down)

    def kv_a_copies(step):
        worker, device, here = place.worker_at(step)
        mine = place.span(place.pos * length)
        move(
            packed.at[worker, pl.ds(0, 2)],
            kva.at[1, :, mine],
            send.at[0, step],
            recv.at[0, place.pos],
            device,
            here,
        )
    def kv_b_copies(step):
        worker, device, here = place.worker_at(step)
        head_b = first_b + worker // 2
        whole = worker % 2 == place.core
        lent = jnp.logical_not(whole) & place.lends(place.core, place.head)

        @pl.when(whole)
        def _():
            move(
                packed.at[head_b, pl.ds(0, 2)],
                kvb.at[1, :, place.span(place.core * TILE_TOK + place.head * length)],
                send.at[1, step],
                recv.at[1, place.pos],
                device,
                here,
            )

        @pl.when(lent)
        def _():
            move(
                packed.at[head_b, pl.ds(0, 2), pl.ds(place.lent_from(place.core), place.piece)],
                kvb.at[1, :, pl.ds(place.lent_to(place.core, place.head), place.piece)],
                send.at[1, step],
                recv.at[1, place.pos],
                device,
                here,
            )

    def qg_a_copies(step):
        worker, device, here = place.worker_at(step)
        mine = place.span(place.pos * length)
        move(
            packed.at[worker, pl.ds(2, 2)],
            qga.at[:, mine],
            send.at[2, step],
            recv.at[2, place.pos],
            device,
            here,
        )

    def qg_b_copies(step):
        worker, device, here = place.worker_at(step)

        @pl.when(worker % 2 == place.core)
        def _():
            move(
                packed.at[first_b + worker // 2, pl.ds(2, 2)],
                qgb.at[:, place.span(place.head * length)],
                send.at[3, step],
                recv.at[3, place.pos],
                device,
                here,
            )

    for copies in (kv_a_copies, qg_a_copies, kv_b_copies, qg_b_copies):
        for step in range(steps):
            copies(step)

    for acc in (acc_a, acc_b):
        acc[...] = jnp.zeros_like(acc)

    def pass_on(ref, part, sems_out, sems_in):
        own = ref.at[1] if part is None else ref.at[1, :, part]
        for way, (exists, tile, slot) in enumerate(
            ((place.has_down, place.tile_down, 0), (place.has_up, place.tile_up, 2))
        ):
            there = ref.at[slot] if part is None else ref.at[slot, :, part]

            @pl.when(exists)
            def _():
                pltpu.make_async_remote_copy(
                    src_ref=own,
                    dst_ref=there,
                    send_sem=sems_out(way),
                    recv_sem=sems_in(way),
                    device_id=(tile, place.head),
                    device_id_type=MESH,
                ).start()

    for step in range(steps):
        pos, core, head, _, _ = place.owner_at(step)
        part = place.span(pos * length)
        wait_in(kva.at[1, :, part], recv.at[0, pos])
        pass_on(
            kva,
            part,
            lambda way: row_send.at[way, pos],
            lambda way: row_recv.at[way, pos],
        )

    def turn(kv, trans, dr):
        def step_of(i, carry):
            at = pl.ds(pl.multiple_of(i * TILE_TOK, TILE_TOK), TILE_TOK)
            for j in range(2):
                trans[dr, j, :, at] = kv[rows[dr], j, at].T
            return carry

        lax.fori_loop(0, kv.shape[2] // TILE_TOK, step_of, 0)

    turn(kva, trans_a, 1)
    for step in range(steps):
        pos = place.owner_at(step)[0]
        wait_in(qga.at[:, place.span(pos * length)], recv.at[2, pos])
    for way, slot in enumerate((0, 2)):
        @pl.when((place.has_up, place.has_down)[way])
        def _():
            for step in range(steps):
                pos = place.owner_at(step)[0]
                wait_in(kva.at[slot, :, place.span(pos * length)], row_recv.at[way, pos])

    turn(kva, trans_a, 0)
    turn(kva, trans_a, 2)

    def unit(i, start, col, base, kv, qg, aq, trans, acc):
        here = pl.ds(pl.multiple_of(i * TILE_TOK, TILE_TOK), TILE_TOK)
        at = pl.ds(pl.multiple_of(start * TILE_TOK, TILE_TOK), WINDOW)
        q, g = qg[0, here], qg[1, here]
        ok = []
        for dr in range(3):
            for j in range(3):
                away = base + start + j - col
                near = (away >= -1) & (away <= 1)
                ok.append(near if dr == 1 else near & row_ok[dr])
        parts = [slice(j * TILE_TOK, (j + 1) * TILE_TOK) for j in range(3)]
        over_lanes = (((1,), (1,)), ((), ()))
        top = jnp.full((1, TILE_TOK), -BIG, f32)
        for dr in range(3):
            s = lax.dot_general(kv[rows[dr], 0, at], q, over_lanes, preferred_element_type=f32)
            probs[dr] = s
            for j in range(3):
                best = jnp.max(s[parts[j]], axis=0, keepdims=True)
                top = jnp.maximum(top, jnp.where(ok[3 * dr + j], best, -BIG))
        top = top * to_log2
        total = jnp.zeros((1, TILE_TOK), f32)
        att = jnp.zeros((HEAD_DIM, TILE_TOK), f32)
        for dr in range(3):
            halves = []
            for j in range(3):
                p = jnp.exp2(probs[dr, parts[j]] * to_log2 - jnp.where(ok[3 * dr + j], top, BIG))
                probs[dr, parts[j]] = p
                total = total + jnp.sum(p, axis=0, keepdims=True)
                halves.append(p.astype(jnp.bfloat16))
            att = att + jnp.dot(
                trans[dr, 1, :, at], jnp.concatenate(halves, axis=0), preferred_element_type=f32
            )
        inverse = 1.0 / total
        att = (att * inverse).astype(jnp.bfloat16)
        aq[0, here] = att.T
        dots = jnp.sum(att.astype(f32) * g.T.astype(f32), axis=0, keepdims=True)
        dq = jnp.zeros((HEAD_DIM, TILE_TOK), f32)
        for dr in range(3):
            w = probs[dr] * inverse
            dp = lax.dot_general(kv[rows[dr], 1, at], g, over_lanes, preferred_element_type=f32)
            ds = (w * (dp - dots)).astype(jnp.bfloat16)
            acc[dr, 1, at] += jnp.dot(w.astype(jnp.bfloat16), g, preferred_element_type=f32)
            acc[dr, 0, at] += jnp.dot(ds, q, preferred_element_type=f32)
            dq = dq + jnp.dot(trans[dr, 0, :, at], ds, preferred_element_type=f32)
        aq[1, here] = (dq * INV_ROOT).T.astype(jnp.bfloat16)

    def unit_a(i, carry):
        last = GRID_COLS - 1
        start = i - 1 + (last - i) // last - i // last
        unit(i, start, i, 0, kva, qga, aqa, trans_a, acc_a)
        return carry

    def unit_b(i, carry):
        last = GRID_COLS // 2 - 1
        start = i - 1 + side + (1 - side) * ((last - i) // last) - side * (i // last)
        col = i + side * (GRID_COLS // 2)
        unit(i, start, col, side * last, kvb, qgb, aqb, trans_b, acc_b)
        return carry

    ways = ((place.has_up, place.tile_up), (place.has_down, place.tile_down))

    def return_rows(kind, acc, far, got):
        for way in range(2):
            for j, scale in enumerate((INV_ROOT, 1.0)):
                far[way, j] = (acc[2 * way, j] * scale).astype(jnp.bfloat16)
        for way, (exists, tile) in enumerate(ways):
            @pl.when(exists)
            def _():
                pltpu.make_async_remote_copy(
                    src_ref=far.at[way],
                    dst_ref=got.at[way],
                    send_sem=ret_send.at[way, kind],
                    recv_sem=ret_recv.at[way, kind],
                    device_id=(tile, place.head),
                    device_id_type=MESH,
                ).start()

    def add_rows(kind, acc, got, total):
        for way, exists in enumerate((place.has_down, place.has_up)):
            @pl.when(exists)
            def _():
                wait_in(got.at[way], ret_recv.at[way, kind])

            @unless(exists)
            def _():
                got[way] = jnp.zeros(got.shape[1:], got.dtype)

        def add(i, carry):
            at = pl.ds(pl.multiple_of(i * TILE_TOK, TILE_TOK), TILE_TOK)
            for j, scale in enumerate((INV_ROOT, 1.0)):
                total[j, at] = (
                    acc[1, j, at] * scale
                    + got[0, j, at].astype(f32)
                    + got[1, j, at].astype(f32)
                ).astype(jnp.bfloat16)
            return carry

        lax.fori_loop(0, total.shape[1] // TILE_TOK, add, 0)

    def send_back_a(source, at, kind):
        for step in range(steps):
            pos, core, head, device, here = place.owner_at(step)
            move(
                source.at[:, place.span(pos * length)],
                out.at[place.worker, pl.ds(at, 2)],
                back_send.at[kind, step],
                back_recv.at[kind, place.worker],
                device,
                here,
            )

    lax.fori_loop(0, GRID_COLS // 2, unit_a, 0)
    for step in range(steps):
        pos, core, head, _, _ = place.owner_at(step)

        @pl.when(core == side)
        def _():
            wait_in(kvb.at[1, :, place.span(core * TILE_TOK + head * length)], recv.at[1, pos])

        @pl.when((core != side) & place.lends(core, head))
        def _():
            wait_in(kvb.at[1, :, pl.ds(place.lent_to(core, head), place.piece)], recv.at[1, pos])

    pass_on(kvb, None, lambda way: row_send_b.at[way], lambda way: row_recv_b.at[way])

    lax.fori_loop(GRID_COLS // 2, GRID_COLS, unit_a, 0)
    return_rows(0, acc_a, far_a, got_a)
    send_back_a(aqa, 2, 0)

    for step in range(steps):
        pos, core, head, _, _ = place.owner_at(step)

        @pl.when(core == side)
        def _():
            wait_in(qgb.at[:, place.span(head * length)], recv.at[3, pos])

    for way, slot in enumerate((0, 2)):
        @pl.when((place.has_up, place.has_down)[way])
        def _():
            wait_in(kvb.at[slot], row_recv_b.at[way])

    for dr in range(3):
        turn(kvb, trans_b, dr)
    lax.fori_loop(0, GRID_COLS // 2 - 1, unit_b, 0)
    add_rows(0, acc_a, got_a, sum_a)
    send_back_a(sum_a, 0, 2)
    lax.fori_loop(GRID_COLS // 2 - 1, GRID_COLS // 2, unit_b, 0)
    return_rows(1, acc_b, far_b, got_b)

    for step in range(steps):
        pos, core, head, device, here = place.owner_at(step)

        @pl.when(core == side)
        def _():
            move(
                aqb.at[:, place.span(head * length)],
                out.at[head_b, pl.ds(2, 2)],
                back_send.at[1, step],
                back_recv.at[1, place.worker],
                device,
                here,
            )

    add_rows(1, acc_b, got_b, sum_b)
    for step in range(steps):
        pos, core, head, device, here = place.owner_at(step)

        @pl.when(core == side)
        def _():
            move(
                sum_b.at[:, place.span(core * TILE_TOK + head * length)],
                out.at[head_b, pl.ds(0, 2)],
                back_send.at[3, step],
                back_recv.at[3, place.worker],
                device,
                here,
            )

        @pl.when((core != side) & place.lends(core, head))
        def _():
            move(
                sum_b.at[:, pl.ds(place.lent_to(core, head), place.piece)],
                halo.at[place.worker // 2],
                back_send.at[3, step],
                back_recv.at[3, place.worker],
                device,
                here,
            )

    for way, exists in enumerate((place.has_down, place.has_up)):
        @pl.when(exists)
        def _():
            for step in range(steps):
                pos = place.owner_at(step)[0]
                wait_in(kva.at[1, :, place.span(pos * length)], row_send.at[way, pos])
            wait_in(kvb.at[1], row_send_b.at[way])

    for step in range(steps):
        worker, device, here = place.worker_at(step)
        whole = worker % 2 == place.core
        lent = jnp.logical_not(whole) & place.lends(place.core, place.head)
        head_w = first_b + worker // 2

        @unless(here)
        def _():
            wait_in(packed.at[worker, pl.ds(0, 2)], send.at[0, step])
            wait_in(packed.at[worker, pl.ds(2, 2)], send.at[2, step])

            @pl.when(whole)
            def _():
                wait_in(packed.at[head_w, pl.ds(0, 2)], send.at[1, step])
                wait_in(packed.at[head_w, pl.ds(2, 2)], send.at[3, step])

            @pl.when(lent)
            def _():
                wait_in(
                    packed.at[head_w, pl.ds(0, 2), pl.ds(place.lent_from(place.core), place.piece)],
                    send.at[1, step],
                )

    for way, (exists, tile) in enumerate(ways):
        @pl.when(exists)
        def _():
            for kind, far in enumerate((far_a, far_b)):
                wait_in(far.at[way], ret_send.at[way, kind])

    for step in range(steps):
        pos, core, head, device, here = place.owner_at(step)
        part = place.span(pos * length)

        @unless(here)
        def _():
            wait_in(aqa.at[:, part], back_send.at[0, step])
            wait_in(sum_a.at[:, part], back_send.at[2, step])

            @pl.when(core == side)
            def _():
                wait_in(aqb.at[:, place.span(head * length)], back_send.at[1, step])
                wait_in(
                    sum_b.at[:, place.span(core * TILE_TOK + head * length)], back_send.at[3, step]
                )

            @pl.when((core != side) & place.lends(core, head))
            def _():
                wait_in(
                    sum_b.at[:, pl.ds(place.lent_to(core, head), place.piece)], back_send.at[3, step]
                )

    for step in range(steps):
        worker, _, _ = place.worker_at(step)
        wait_in(out.at[worker, pl.ds(2, 2)], back_recv.at[0, worker])
        wait_in(out.at[worker, pl.ds(0, 2)], back_recv.at[2, worker])
        whole = worker % 2 == place.core
        lent = jnp.logical_not(whole) & place.lends(place.core, place.head)

        @pl.when(whole)
        def _():
            wait_in(out.at[first_b + worker // 2, pl.ds(2, 2)], back_recv.at[1, worker])
            wait_in(out.at[first_b + worker // 2, pl.ds(0, 2)], back_recv.at[3, worker])

        @pl.when(lent)
        def _():
            wait_in(halo.at[worker // 2], back_recv.at[3, worker])


def local(head_axis, queries, keys_in, values_in, grad_out, positions):
    length, width = queries.shape
    heads = width // HEAD_DIM
    bf16, f32 = jnp.bfloat16, jnp.float32
    assert heads == 3 * head_axis and 2 * head_axis * length == ROW_TOK and head_axis % 2 == 0
    place = Place(head_axis, length)
    piece = place.piece
    steps = 2 * head_axis
    cosine, sine = angle_tables(positions[0], positions[1])
    any_space = pl.BlockSpec(memory_space=pl.ANY)
    vmem = pl.BlockSpec(memory_space=pltpu.VMEM)
    smem = pl.BlockSpec(memory_space=pltpu.SMEM)
    shape = jax.ShapeDtypeStruct
    dma = pltpu.SemaphoreType.DMA

    packed = pl.pallas_call(
        pack_kernel,
        out_shape=shape((heads, 4, length, HEAD_DIM), bf16),
        in_specs=[vmem] * 6,
        out_specs=vmem,
        compiler_params=pltpu.CompilerParams(vmem_limit_bytes=VMEM_LIMIT),
    )(queries, keys_in, values_in, grad_out, cosine, sine)

    out, halo = pl.pallas_call(
        functools.partial(attend_kernel, head_axis, length),
        out_shape=(
            shape((heads, 4, length, HEAD_DIM), bf16),
            shape((head_axis, 2, piece, HEAD_DIM), bf16),
        ),
        in_specs=[any_space],
        out_specs=[any_space] * 2,
        scratch_shapes=[
            pltpu.VMEM((3, 2, ROW_TOK, HEAD_DIM), bf16),
            pltpu.VMEM((3, 2, BAND_TOK, HEAD_DIM), bf16),
            pltpu.VMEM((2, ROW_TOK, HEAD_DIM), bf16),
            pltpu.VMEM((2, HALF_TOK, HEAD_DIM), bf16),
            pltpu.VMEM((2, ROW_TOK, HEAD_DIM), bf16),
            pltpu.VMEM((2, HALF_TOK, HEAD_DIM), bf16),
            pltpu.VMEM((2, 2, ROW_TOK, HEAD_DIM), bf16),
            pltpu.VMEM((2, 2, BAND_TOK, HEAD_DIM), bf16),
            pltpu.VMEM((2, 2, ROW_TOK, HEAD_DIM), bf16),
            pltpu.VMEM((2, 2, BAND_TOK, HEAD_DIM), bf16),
            pltpu.VMEM((2, ROW_TOK, HEAD_DIM), bf16),
            pltpu.VMEM((2, BAND_TOK, HEAD_DIM), bf16),
            pltpu.VMEM((3, 2, HEAD_DIM, ROW_TOK), bf16),
            pltpu.VMEM((3, 2, HEAD_DIM, BAND_TOK), bf16),
            pltpu.VMEM((3, 2, ROW_TOK, HEAD_DIM), f32),
            pltpu.VMEM((3, 2, BAND_TOK, HEAD_DIM), f32),
            pltpu.VMEM((3, WINDOW, TILE_TOK), f32),
            dma((4, steps)),
            dma((4, steps)),
            dma((2, steps)),
            dma((2, steps)),
            dma((2,)),
            dma((2,)),
            dma((4, steps)),
            dma((4, steps)),
            dma((2, 2)),
            dma((2, 2)),
        ],
        compiler_params=pltpu.CompilerParams(
            collective_id=0, has_side_effects=True, vmem_limit_bytes=VMEM_LIMIT
        ),
    )(packed)

    lends = place.lends(place.core, place.head)
    halo_flags = jnp.stack([lends & (place.core == 1), lends & (place.core == 0)]).astype(jnp.int32)
    return pl.pallas_call(
        unpack_kernel,
        out_shape=(shape((length, width), bf16),) * 4,
        in_specs=[smem] + [vmem] * 4,
        out_specs=[vmem] * 4,
        compiler_params=pltpu.CompilerParams(vmem_limit_bytes=VMEM_LIMIT),
    )(halo_flags, out, halo, cosine, sine)


def solution(mesh):
    tokens = P(("tile", "head"), None)
    return jax.shard_map(
        functools.partial(local, mesh.shape["head"]),
        mesh=mesh,
        in_specs=(tokens, tokens, tokens, tokens, P(None, ("tile", "head"))),
        out_specs=(tokens, tokens, tokens, tokens),
        check_vma=False,
    )
```

```python
import functools
import math

import jax
import jax.numpy as jnp
from jax import lax
from jax.experimental import pallas as pl
from jax.experimental.pallas import tpu as pltpu
from jax.sharding import PartitionSpec as P

HEAD_DIM = 128
TILE_TOK = 256
GRID_COLS = 8
ROW_TOK = TILE_TOK * GRID_COLS
HALF_TOK = ROW_TOK // 2
BAND_TOK = HALF_TOK + TILE_TOK
WINDOW = 3 * TILE_TOK
THETA = 10000.0
MESH = pl.DeviceIdType.MESH
INV_ROOT = HEAD_DIM ** (-0.5)
VMEM_LIMIT = 56 * 1024 * 1024


def angle_tables(row_ids, col_ids):
    turned = 7 * HEAD_DIM // 16
    unturned = HEAD_DIM - 2 * turned
    slot_ids = lax.iota(jnp.int32, HEAD_DIM)
    offset = slot_ids - unturned
    by_column = offset >= turned
    within = jnp.where(by_column, offset - turned, offset)
    paired = jnp.maximum(within, 0) // 2
    frequency = jnp.exp(paired.astype(jnp.float32) * (-2.0 * math.log(THETA) / turned))
    chosen = jnp.where(by_column[None, :], col_ids[:, None], row_ids[:, None]).astype(jnp.float32)
    angles = chosen * frequency[None, :]
    active = (offset >= 0)[None, :]
    cosine = jnp.where(active, jnp.cos(angles), 1.0)
    parity = jnp.where(within % 2 == 0, -1.0, 1.0)
    signed_sine = jnp.where(active, jnp.sin(angles) * parity[None, :], 0.0)
    return (cosine, signed_sine)


def swapped(x):
    lane = lax.broadcasted_iota(jnp.int32, x.shape, 1)
    after = pltpu.roll(x, HEAD_DIM - 1, 1)
    before = pltpu.roll(x, 1, 1)
    return jnp.where(lane % 2 == 0, after, before)


def pack_kernel(q_ref, k_ref, v_ref, g_ref, cos_ref, sin_ref, packed):
    cosine, sine = cos_ref[...], sin_ref[...]
    for slot, ref in ((0, k_ref), (2, q_ref)):
        x = ref[...].astype(jnp.float32)
        packed[0, slot] = (x * cosine + swapped(x) * sine).astype(jnp.bfloat16)
    packed[0, 1] = v_ref[...]
    packed[0, 3] = g_ref[...]


def unpack_kernel(flag_ref, out_ref, halo_ref, cos_ref, sin_ref, att_ref, dq_ref, dk_ref, dv_ref):
    cosine, sine = cos_ref[...], sin_ref[...]
    length, piece = out_ref.shape[2], halo_ref.shape[2]

    def back(x):
        return (x * cosine + swapped(x * sine)).astype(jnp.bfloat16)

    shared = pl.program_id(0) >= flag_ref[2]
    att_ref[...] = out_ref[0, 2]
    dq_ref[...] = back(out_ref[0, 3].astype(jnp.float32))
    pair = [out_ref[0, i].astype(jnp.float32) for i in range(2)]
    for i in range(2):
        extra = halo_ref[0, i].astype(jnp.float32)
        first = jnp.where(shared & (flag_ref[0] > 0), extra, 0.0)
        last = jnp.where(shared & (flag_ref[1] > 0), extra, 0.0)
        if piece == length:
            pair[i] = pair[i] + first + last
        else:
            gap = jnp.zeros((length - piece, HEAD_DIM), jnp.float32)
            pair[i] = (
                pair[i]
                + jnp.concatenate([first, gap], axis=0)
                + jnp.concatenate([gap, last], axis=0)
            )
    dk_ref[...] = back(pair[0])
    dv_ref[...] = pair[1].astype(jnp.bfloat16)


class Place:
    def __init__(self, head_axis, length):
        self.tile = lax.axis_index("tile")
        self.head = lax.axis_index("head")
        self.heads = head_axis
        self.length = length
        self.piece = min(length, TILE_TOK)
        self.pieces = TILE_TOK // self.piece
        self.plane = self.tile // 4
        self.x = (self.tile // 2) % 2
        self.core = self.tile % 2
        self.pos = self.core * head_axis + self.head
        self.worker = self.x * head_axis + self.head
        self.row = 2 * self.plane + self.core
        self.rows = lax.axis_size("tile") // 2
        self.has_up = self.row > 0
        self.has_down = self.row < self.rows - 1
        self.tile_up = self.tile - 3 + 2 * self.core
        self.tile_down = self.tile + 1 + 2 * self.core

    def worker_at(self, step):
        worker = (self.worker + step) % (2 * self.heads)
        x, head = worker // self.heads, worker % self.heads
        tile = self.plane * 4 + x * 2 + self.x
        here = (tile == self.tile) & (head == self.head)
        return worker, (tile, head), here

    def owner_at(self, step):
        pos = (self.pos + step) % (2 * self.heads)
        core, head = pos // self.heads, pos % self.heads
        tile = self.plane * 4 + self.core * 2 + core
        here = (tile == self.tile) & (head == self.head)
        return pos, core, head, (tile, head), here

    def lends(self, core, head):
        return jnp.where(core == 1, head, self.heads - 1 - head) < self.pieces

    def lent_from(self, core):
        return pl.multiple_of((1 - core) * (self.length - self.piece), self.piece)

    def lent_to(self, core, head):
        low = (head - (self.heads - self.pieces)) * self.piece
        high = HALF_TOK + head * self.piece
        return pl.multiple_of(core * high + (1 - core) * low, self.piece)

    def span(self, start, size=None):
        size = self.length if size is None else size
        return pl.ds(pl.multiple_of(start, self.piece), size)


def move(src, dst, send_sem, recv_sem, device, here):
    remote = pltpu.make_async_remote_copy(
        src_ref=src,
        dst_ref=dst,
        send_sem=send_sem,
        recv_sem=recv_sem,
        device_id=device,
        device_id_type=MESH,
    )

    @pl.when(here)
    def _():
        pltpu.make_async_copy(src, dst, recv_sem).start()

    @pl.when(jnp.logical_not(here))
    def _():
        remote.start()

    return remote


def wait_in(dst, sem):
    pltpu.make_async_copy(dst, dst, sem).wait()


def unless(flag):
    return pl.when(jnp.logical_not(flag))


def greet(place, devices):
    barrier = pltpu.get_barrier_semaphore()

    def tell(device):
        pl.semaphore_signal(barrier, inc=1, device_id=device, device_id_type=MESH)

    for device, here in devices:
        @unless(here)
        def _():
            tell(device)

    @pl.when(place.has_up)
    def _():
        tell((place.tile_up, place.head))

    @pl.when(place.has_down)
    def _():
        tell((place.tile_down, place.head))

    own = (place.x == place.core).astype(jnp.int32)
    ends = place.has_up.astype(jnp.int32) + place.has_down.astype(jnp.int32)
    pl.semaphore_wait(barrier, len(devices) - 2 * own + ends)


BIG = 1e30


def attend_kernel(
    head_axis,
    length,
    packed,
    out,
    halo,
    kva,
    kvb,
    qga,
    qgb,
    aqa,
    aqb,
    far_a,
    far_b,
    got_a,
    got_b,
    sum_a,
    sum_b,
    trans_a,
    trans_b,
    acc_a,
    acc_b,
    probs,
    send,
    recv,
    row_send,
    row_recv,
    row_send_b,
    row_recv_b,
    back_send,
    back_recv,
    ret_send,
    ret_recv,
):
    place = Place(head_axis, length)
    steps = 2 * head_axis
    first_b = 2 * head_axis
    greet(
        place,
        [place.owner_at(s)[3:5] for s in range(steps)]
        + [place.worker_at(s)[1:3] for s in range(steps)],
    )
    side = place.worker % 2
    head_b = first_b + place.worker // 2
    to_log2 = INV_ROOT / math.log(2.0)
    f32 = jnp.float32
    row_ok = (place.has_up, True, place.has_down)
    up = (place.row + place.rows - 1) // place.rows
    down = 1 - place.row // (place.rows - 1)
    rows = (1 - up, 1, 1 + down)

    def kv_a_copies(step):
        worker, device, here = place.worker_at(step)
        mine = place.span(place.pos * length)
        move(
            packed.at[worker, pl.ds(0, 2)],
            kva.at[1, :, mine],
            send.at[0, step],
            recv.at[0, place.pos],
            device,
            here,
        )
    def kv_b_copies(step):
        worker, device, here = place.worker_at(step)
        head_b = first_b + worker // 2
        whole = worker % 2 == place.core
        lent = jnp.logical_not(whole) & place.lends(place.core, place.head)

        @pl.when(whole)
        def _():
            move(
                packed.at[head_b, pl.ds(0, 2)],
                kvb.at[1, :, place.span(place.core * TILE_TOK + place.head * length)],
                send.at[1, step],
                recv.at[1, place.pos],
                device,
                here,
            )

        @pl.when(lent)
        def _():
            move(
                packed.at[head_b, pl.ds(0, 2), pl.ds(place.lent_from(place.core), place.piece)],
                kvb.at[1, :, pl.ds(place.lent_to(place.core, place.head), place.piece)],
                send.at[1, step],
                recv.at[1, place.pos],
                device,
                here,
            )

    def qg_a_copies(step):
        worker, device, here = place.worker_at(step)
        mine = place.span(place.pos * length)
        move(
            packed.at[worker, pl.ds(2, 2)],
            qga.at[:, mine],
            send.at[2, step],
            recv.at[2, place.pos],
            device,
            here,
        )

    def qg_b_copies(step):
        worker, device, here = place.worker_at(step)

        @pl.when(worker % 2 == place.core)
        def _():
            move(
                packed.at[first_b + worker // 2, pl.ds(2, 2)],
                qgb.at[:, place.span(place.head * length)],
                send.at[3, step],
                recv.at[3, place.pos],
                device,
                here,
            )

    for copies in (kv_a_copies, qg_a_copies, kv_b_copies, qg_b_copies):
        for step in range(steps):
            copies(step)

    for acc in (acc_a, acc_b):
        acc[...] = jnp.zeros_like(acc)

    def pass_on(ref, part, sems_out, sems_in):
        own = ref.at[1] if part is None else ref.at[1, :, part]
        for way, (exists, tile, slot) in enumerate(
            ((place.has_down, place.tile_down, 0), (place.has_up, place.tile_up, 2))
        ):
            there = ref.at[slot] if part is None else ref.at[slot, :, part]

            @pl.when(exists)
            def _():
                pltpu.make_async_remote_copy(
                    src_ref=own,
                    dst_ref=there,
                    send_sem=sems_out(way),
                    recv_sem=sems_in(way),
                    device_id=(tile, place.head),
                    device_id_type=MESH,
                ).start()

    for step in range(steps):
        pos, core, head, _, _ = place.owner_at(step)
        part = place.span(pos * length)
        wait_in(kva.at[1, :, part], recv.at[0, pos])
        pass_on(
            kva,
            part,
            lambda way: row_send.at[way, pos],
            lambda way: row_recv.at[way, pos],
        )

    def turn(kv, trans, dr):
        def step_of(i, carry):
            at = pl.ds(pl.multiple_of(i * TILE_TOK, TILE_TOK), TILE_TOK)
            for j in range(2):
                trans[dr, j, :, at] = kv[rows[dr], j, at].T
            return carry

        lax.fori_loop(0, kv.shape[2] // TILE_TOK, step_of, 0)

    turn(kva, trans_a, 1)
    for step in range(steps):
        pos = place.owner_at(step)[0]
        wait_in(qga.at[:, place.span(pos * length)], recv.at[2, pos])
    for way, slot in enumerate((0, 2)):
        @pl.when((place.has_up, place.has_down)[way])
        def _():
            for step in range(steps):
                pos = place.owner_at(step)[0]
                wait_in(kva.at[slot, :, place.span(pos * length)], row_recv.at[way, pos])

    turn(kva, trans_a, 0)
    turn(kva, trans_a, 2)

    def unit(i, start, col, base, kv, qg, aq, trans, acc):
        here = pl.ds(pl.multiple_of(i * TILE_TOK, TILE_TOK), TILE_TOK)
        at = pl.ds(pl.multiple_of(start * TILE_TOK, TILE_TOK), WINDOW)
        q, g = qg[0, here], qg[1, here]
        ok = []
        for dr in range(3):
            for j in range(3):
                away = base + start + j - col
                near = (away >= -1) & (away <= 1)
                ok.append(near if dr == 1 else near & row_ok[dr])
        parts = [slice(j * TILE_TOK, (j + 1) * TILE_TOK) for j in range(3)]
        over_lanes = (((1,), (1,)), ((), ()))
        top = jnp.full((1, TILE_TOK), -BIG, f32)
        for dr in range(3):
            s = lax.dot_general(kv[rows[dr], 0, at], q, over_lanes, preferred_element_type=f32)
            probs[dr] = s
            for j in range(3):
                best = jnp.max(s[parts[j]], axis=0, keepdims=True)
                top = jnp.maximum(top, jnp.where(ok[3 * dr + j], best, -BIG))
        top = top * to_log2
        total = jnp.zeros((1, TILE_TOK), f32)
        att = jnp.zeros((HEAD_DIM, TILE_TOK), f32)
        for dr in range(3):
            halves = []
            for j in range(3):
                p = jnp.exp2(probs[dr, parts[j]] * to_log2 - jnp.where(ok[3 * dr + j], top, BIG))
                probs[dr, parts[j]] = p
                total = total + jnp.sum(p, axis=0, keepdims=True)
                halves.append(p.astype(jnp.bfloat16))
            att = att + jnp.dot(
                trans[dr, 1, :, at], jnp.concatenate(halves, axis=0), preferred_element_type=f32
            )
        inverse = 1.0 / total
        att = (att * inverse).astype(jnp.bfloat16)
        aq[0, here] = att.T
        dots = jnp.sum(att.astype(f32) * g.T.astype(f32), axis=0, keepdims=True)
        dq = jnp.zeros((HEAD_DIM, TILE_TOK), f32)
        for dr in range(3):
            w = probs[dr] * inverse
            dp = lax.dot_general(kv[rows[dr], 1, at], g, over_lanes, preferred_element_type=f32)
            ds = (w * (dp - dots)).astype(jnp.bfloat16)
            acc[dr, 1, at] += jnp.dot(w.astype(jnp.bfloat16), g, preferred_element_type=f32)
            acc[dr, 0, at] += jnp.dot(ds, q, preferred_element_type=f32)
            dq = dq + jnp.dot(trans[dr, 0, :, at], ds, preferred_element_type=f32)
        aq[1, here] = (dq * INV_ROOT).T.astype(jnp.bfloat16)

    def unit_a(i, carry):
        last = GRID_COLS - 1
        start = i - 1 + (last - i) // last - i // last
        unit(i, start, i, 0, kva, qga, aqa, trans_a, acc_a)
        return carry

    def unit_b(i, carry):
        last = GRID_COLS // 2 - 1
        start = i - 1 + side + (1 - side) * ((last - i) // last) - side * (i // last)
        col = i + side * (GRID_COLS // 2)
        unit(i, start, col, side * last, kvb, qgb, aqb, trans_b, acc_b)
        return carry

    ways = ((place.has_up, place.tile_up), (place.has_down, place.tile_down))

    def return_rows(kind, acc, far, got):
        for way in range(2):
            for j, scale in enumerate((INV_ROOT, 1.0)):
                far[way, j] = (acc[2 * way, j] * scale).astype(jnp.bfloat16)
        for way, (exists, tile) in enumerate(ways):
            @pl.when(exists)
            def _():
                pltpu.make_async_remote_copy(
                    src_ref=far.at[way],
                    dst_ref=got.at[way],
                    send_sem=ret_send.at[way, kind],
                    recv_sem=ret_recv.at[way, kind],
                    device_id=(tile, place.head),
                    device_id_type=MESH,
                ).start()

    def add_rows(kind, acc, got, total):
        for way, exists in enumerate((place.has_down, place.has_up)):
            @pl.when(exists)
            def _():
                wait_in(got.at[way], ret_recv.at[way, kind])

            @unless(exists)
            def _():
                got[way] = jnp.zeros(got.shape[1:], got.dtype)

        def add(i, carry):
            at = pl.ds(pl.multiple_of(i * TILE_TOK, TILE_TOK), TILE_TOK)
            for j, scale in enumerate((INV_ROOT, 1.0)):
                total[j, at] = (
                    acc[1, j, at] * scale
                    + got[0, j, at].astype(f32)
                    + got[1, j, at].astype(f32)
                ).astype(jnp.bfloat16)
            return carry

        lax.fori_loop(0, total.shape[1] // TILE_TOK, add, 0)

    def send_back_a(source, at, kind):
        for step in range(steps):
            pos, core, head, device, here = place.owner_at(step)
            move(
                source.at[:, place.span(pos * length)],
                out.at[place.worker, pl.ds(at, 2)],
                back_send.at[kind, step],
                back_recv.at[kind, place.worker],
                device,
                here,
            )

    lax.fori_loop(0, GRID_COLS // 2, unit_a, 0)
    for step in range(steps):
        pos, core, head, _, _ = place.owner_at(step)

        @pl.when(core == side)
        def _():
            wait_in(kvb.at[1, :, place.span(core * TILE_TOK + head * length)], recv.at[1, pos])

        @pl.when((core != side) & place.lends(core, head))
        def _():
            wait_in(kvb.at[1, :, pl.ds(place.lent_to(core, head), place.piece)], recv.at[1, pos])

    pass_on(kvb, None, lambda way: row_send_b.at[way], lambda way: row_recv_b.at[way])

    lax.fori_loop(GRID_COLS // 2, GRID_COLS, unit_a, 0)
    return_rows(0, acc_a, far_a, got_a)
    send_back_a(aqa, 2, 0)

    for step in range(steps):
        pos, core, head, _, _ = place.owner_at(step)

        @pl.when(core == side)
        def _():
            wait_in(qgb.at[:, place.span(head * length)], recv.at[3, pos])

    for way, slot in enumerate((0, 2)):
        @pl.when((place.has_up, place.has_down)[way])
        def _():
            wait_in(kvb.at[slot], row_recv_b.at[way])

    for dr in range(3):
        turn(kvb, trans_b, dr)
    lax.fori_loop(0, GRID_COLS // 2 - 1, unit_b, 0)
    add_rows(0, acc_a, got_a, sum_a)
    send_back_a(sum_a, 0, 2)
    lax.fori_loop(GRID_COLS // 2 - 1, GRID_COLS // 2, unit_b, 0)
    return_rows(1, acc_b, far_b, got_b)

    for step in range(steps):
        pos, core, head, device, here = place.owner_at(step)

        @pl.when(core == side)
        def _():
            move(
                aqb.at[:, place.span(head * length)],
                out.at[head_b, pl.ds(2, 2)],
                back_send.at[1, step],
                back_recv.at[1, place.worker],
                device,
                here,
            )

    add_rows(1, acc_b, got_b, sum_b)
    for step in range(steps):
        pos, core, head, device, here = place.owner_at(step)

        @pl.when(core == side)
        def _():
            move(
                sum_b.at[:, place.span(core * TILE_TOK + head * length)],
                out.at[head_b, pl.ds(0, 2)],
                back_send.at[3, step],
                back_recv.at[3, place.worker],
                device,
                here,
            )

        @pl.when((core != side) & place.lends(core, head))
        def _():
            move(
                sum_b.at[:, pl.ds(place.lent_to(core, head), place.piece)],
                halo.at[place.worker // 2],
                back_send.at[3, step],
                back_recv.at[3, place.worker],
                device,
                here,
            )

    for way, exists in enumerate((place.has_down, place.has_up)):
        @pl.when(exists)
        def _():
            for step in range(steps):
                pos = place.owner_at(step)[0]
                wait_in(kva.at[1, :, place.span(pos * length)], row_send.at[way, pos])
            wait_in(kvb.at[1], row_send_b.at[way])

    for step in range(steps):
        worker, device, here = place.worker_at(step)
        whole = worker % 2 == place.core
        lent = jnp.logical_not(whole) & place.lends(place.core, place.head)
        head_w = first_b + worker // 2

        @unless(here)
        def _():
            wait_in(packed.at[worker, pl.ds(0, 2)], send.at[0, step])
            wait_in(packed.at[worker, pl.ds(2, 2)], send.at[2, step])

            @pl.when(whole)
            def _():
                wait_in(packed.at[head_w, pl.ds(0, 2)], send.at[1, step])
                wait_in(packed.at[head_w, pl.ds(2, 2)], send.at[3, step])

            @pl.when(lent)
            def _():
                wait_in(
                    packed.at[head_w, pl.ds(0, 2), pl.ds(place.lent_from(place.core), place.piece)],
                    send.at[1, step],
                )

    for way, (exists, tile) in enumerate(ways):
        @pl.when(exists)
        def _():
            for kind, far in enumerate((far_a, far_b)):
                wait_in(far.at[way], ret_send.at[way, kind])

    for step in range(steps):
        pos, core, head, device, here = place.owner_at(step)
        part = place.span(pos * length)

        @unless(here)
        def _():
            wait_in(aqa.at[:, part], back_send.at[0, step])
            wait_in(sum_a.at[:, part], back_send.at[2, step])

            @pl.when(core == side)
            def _():
                wait_in(aqb.at[:, place.span(head * length)], back_send.at[1, step])
                wait_in(
                    sum_b.at[:, place.span(core * TILE_TOK + head * length)], back_send.at[3, step]
                )

            @pl.when((core != side) & place.lends(core, head))
            def _():
                wait_in(
                    sum_b.at[:, pl.ds(place.lent_to(core, head), place.piece)], back_send.at[3, step]
                )

    for step in range(steps):
        worker, _, _ = place.worker_at(step)
        wait_in(out.at[worker, pl.ds(2, 2)], back_recv.at[0, worker])
        wait_in(out.at[worker, pl.ds(0, 2)], back_recv.at[2, worker])
        whole = worker % 2 == place.core
        lent = jnp.logical_not(whole) & place.lends(place.core, place.head)

        @pl.when(whole)
        def _():
            wait_in(out.at[first_b + worker // 2, pl.ds(2, 2)], back_recv.at[1, worker])
            wait_in(out.at[first_b + worker // 2, pl.ds(0, 2)], back_recv.at[3, worker])

        @pl.when(lent)
        def _():
            wait_in(halo.at[worker // 2], back_recv.at[3, worker])


def local(head_axis, queries, keys_in, values_in, grad_out, positions):
    length, width = queries.shape
    heads = width // HEAD_DIM
    bf16, f32 = jnp.bfloat16, jnp.float32
    assert heads == 3 * head_axis and 2 * head_axis * length == ROW_TOK and head_axis % 2 == 0
    place = Place(head_axis, length)
    piece = place.piece
    steps = 2 * head_axis
    cosine, sine = angle_tables(positions[0], positions[1])
    any_space = pl.BlockSpec(memory_space=pl.ANY)
    by_head = pl.BlockSpec((length, HEAD_DIM), lambda h: (0, h))
    table = pl.BlockSpec((length, HEAD_DIM), lambda h: (0, 0))
    smem = pl.BlockSpec(memory_space=pltpu.SMEM)
    shape = jax.ShapeDtypeStruct
    dma = pltpu.SemaphoreType.DMA

    packed = pl.pallas_call(
        pack_kernel,
        out_shape=shape((heads, 4, length, HEAD_DIM), bf16),
        grid=(heads,),
        in_specs=[by_head] * 4 + [table] * 2,
        out_specs=pl.BlockSpec((1, 4, length, HEAD_DIM), lambda h: (h, 0, 0, 0)),
        compiler_params=pltpu.CompilerParams(vmem_limit_bytes=VMEM_LIMIT),
    )(queries, keys_in, values_in, grad_out, cosine, sine)

    out, halo = pl.pallas_call(
        functools.partial(attend_kernel, head_axis, length),
        out_shape=(
            shape((heads, 4, length, HEAD_DIM), bf16),
            shape((head_axis, 2, piece, HEAD_DIM), bf16),
        ),
        in_specs=[any_space],
        out_specs=[any_space] * 2,
        scratch_shapes=[
            pltpu.VMEM((3, 2, ROW_TOK, HEAD_DIM), bf16),
            pltpu.VMEM((3, 2, BAND_TOK, HEAD_DIM), bf16),
            pltpu.VMEM((2, ROW_TOK, HEAD_DIM), bf16),
            pltpu.VMEM((2, HALF_TOK, HEAD_DIM), bf16),
            pltpu.VMEM((2, ROW_TOK, HEAD_DIM), bf16),
            pltpu.VMEM((2, HALF_TOK, HEAD_DIM), bf16),
            pltpu.VMEM((2, 2, ROW_TOK, HEAD_DIM), bf16),
            pltpu.VMEM((2, 2, BAND_TOK, HEAD_DIM), bf16),
            pltpu.VMEM((2, 2, ROW_TOK, HEAD_DIM), bf16),
            pltpu.VMEM((2, 2, BAND_TOK, HEAD_DIM), bf16),
            pltpu.VMEM((2, ROW_TOK, HEAD_DIM), bf16),
            pltpu.VMEM((2, BAND_TOK, HEAD_DIM), bf16),
            pltpu.VMEM((3, 2, HEAD_DIM, ROW_TOK), bf16),
            pltpu.VMEM((3, 2, HEAD_DIM, BAND_TOK), bf16),
            pltpu.VMEM((3, 2, ROW_TOK, HEAD_DIM), f32),
            pltpu.VMEM((3, 2, BAND_TOK, HEAD_DIM), f32),
            pltpu.VMEM((3, WINDOW, TILE_TOK), f32),
            dma((4, steps)),
            dma((4, steps)),
            dma((2, steps)),
            dma((2, steps)),
            dma((2,)),
            dma((2,)),
            dma((4, steps)),
            dma((4, steps)),
            dma((2, 2)),
            dma((2, 2)),
        ],
        compiler_params=pltpu.CompilerParams(
            collective_id=0, has_side_effects=True, vmem_limit_bytes=VMEM_LIMIT
        ),
    )(packed)

    lends = place.lends(place.core, place.head)
    first_b = heads - head_axis
    halo_flags = jnp.stack(
        [lends & (place.core == 1), lends & (place.core == 0), jnp.int32(first_b)]
    ).astype(jnp.int32)
    return pl.pallas_call(
        unpack_kernel,
        out_shape=(shape((length, width), bf16),) * 4,
        grid=(heads,),
        in_specs=[
            smem,
            pl.BlockSpec((1, 4, length, HEAD_DIM), lambda h: (h, 0, 0, 0)),
            pl.BlockSpec((1, 2, piece, HEAD_DIM), lambda h: (jnp.maximum(h - first_b, 0), 0, 0, 0)),
            table,
            table,
        ],
        out_specs=[by_head] * 4,
        compiler_params=pltpu.CompilerParams(vmem_limit_bytes=VMEM_LIMIT),
    )(halo_flags, out, halo, cosine, sine)


def solution(mesh):
    tokens = P(("tile", "head"), None)
    return jax.shard_map(
        functools.partial(local, mesh.shape["head"]),
        mesh=mesh,
        in_specs=(tokens, tokens, tokens, tokens, P(None, ("tile", "head"))),
        out_specs=(tokens, tokens, tokens, tokens),
        check_vma=False,
    )
```
